32 devices in a mesh: groups: 2 (over y), sketch: 4 (over z), context: 2 (over x), example: 2 (over core).
Axes of the slice: x: 2, y: 2, z: 4, core: 2. Of those that a mesh axis runs over, the one named last changes fastest.
Arguments:
- activations: bfloat16 [8, 4096, 512], P('groups', ('sketch', 'context')), parts along dimension 0, may hold values from -6 to 6
- out_grads: bfloat16 [8, 4096, 512], P('groups', ('sketch', 'example')), parts along dimension 0, may hold values from -6 to 6
- sign_bits: int32 [4, 2, 512, 2, 128], P(None, 'context', None, 'example'), may hold values from 0 to 65535
- keep_cols: int32 [128], replicated, may hold values from 0 to 31
- row_start: int32 [128], P(('context', 'example')), may hold values from 0 to 4095
- row_step: int32 [128], P(('context', 'example')), may hold values from 0 to 2047
- val_sketch: float32 [64, 8192], P('sketch', ('context', 'example')), may hold values from -6 to 6
Outputs:
- scores: float32 [8, 64], P(('groups', 'sketch')), parts along dimension 0
The draws below stay inside these ranges and needn't reach their ends.
There are 2 independent parts, one for each index of `groups`. The reference program is written for one: setup_inputs(seed, part) draws one part's arguments, and reference() takes and returns one part's arrays. A program takes and returns all parts, laid end to end along the dimension named above; an argument that names none is the same for every part. Nothing has to cross between parts.
Inputs may be any that keep to these rules, and one draw needn't show every extreme that they name: `sign_bits`: each word holds 16 independent fair sign bits in its low 16 bits.
All inputs are finite; a program needn't handle non-finite values.
Results may differ from the reference program's by a relative error of at most 0.0003.
Values may be sent and summed in bfloat16 or wider, within the bound.
A program may use at most 128 MiB of HBM per device.

```python
import math
import jax
import jax.numpy as jnp
from jax import lax

DI = 4096
DO = 4096
TOKENS = 512
KR = 64
KC = 128
NV = 64
EXAMPLES = 4
RK = 512
WK = 512
KEEP = 8192
N_SKETCH = 4
N_CONTEXT = 2
N_EXAMPLE = 2


def place_ends(values, rng, smallest, top_value):
    shape = values.shape
    spot = [jax.random.randint(jax.random.fold_in(rng, axis), (), 0, shape[axis]) for axis in range(len(shape))]
    values = values.at[tuple(spot)].set(smallest)
    longest = shape.index(max(shape))
    spot[longest] = (spot[longest] + 1) % shape[longest]
    return values.at[tuple(spot)].set(top_value)


def level_of(stream_key, extent, shards, low, top_value):
    level = 1.0
    for axis_at, parts in shards:
        heights = jax.random.uniform(jax.random.fold_in(jax.random.fold_in(stream_key, 6), axis_at), (parts,), jnp.float32, low / len(shards), top_value / len(shards))
        level = level * jnp.repeat(jnp.exp(heights), extent[axis_at] // parts).reshape((-1,) + (1,) * (len(extent) - 1 - axis_at))
    return level


def bell_draw(rng, shape, spread, most, pieces=(), kind=jnp.bfloat16):
    result = jax.random.normal(rng, shape, jnp.float32) * spread
    if len(pieces) > 0:
        result = level_of(rng, shape, pieces, -0.22, 0.18) * result
    return jnp.clip(result, min=-most, max=most).astype(kind)


def setup_inputs(seed: int = 0, part: int = 0) -> dict:
    streams_of = jax.random.split(jax.random.key(seed), 8)
    part_splits = jax.random.split(jax.random.fold_in(streams_of[7], part), 8)
    return {
        "activations": bell_draw(part_splits[0], (EXAMPLES, DI, TOKENS), 1.0, 6.0, ((1, 8),)),
        "out_grads": bell_draw(part_splits[1], (EXAMPLES, DO, TOKENS), 1.0, 6.0, ((1, 8),)),
        "sign_bits": place_ends(jax.random.randint(streams_of[2], (N_SKETCH, N_CONTEXT, RK, N_EXAMPLE, N_SKETCH * WK // 16), 0, 65536), jax.random.fold_in(streams_of[2], 1), 0, 65535).astype(jnp.int32),
        "keep_cols": place_ends(jax.random.randint(streams_of[3], (KC,), 0, DO // KC), jax.random.fold_in(streams_of[3], 1), 0, (DO // KC) - 1).astype(jnp.int32),
        "row_start": place_ends(jax.random.randint(streams_of[4], (KC,), 0, DI), jax.random.fold_in(streams_of[4], 1), 0, DI - 1).astype(jnp.int32),
        "row_step": place_ends(jax.random.randint(streams_of[5], (KC,), 0, DI // 2), jax.random.fold_in(streams_of[5], 1), 0, (DI // 2) - 1).astype(jnp.int32),
        "val_sketch": bell_draw(streams_of[6], (NV, KEEP), 1.0, 6.0, ((0, 4), (1, 4)), jnp.float32),
    }


def parity_sign(common, length):
    ones_total = jnp.zeros(common.shape, jnp.int32)
    for bit_place in range(max(length.bit_length() - 1, 1)):
        ones_total = ones_total + jnp.bitwise_and(jnp.right_shift(common, bit_place), 1)
    return (1 - 2 * jnp.bitwise_and(ones_total, 1)).astype(jnp.float32)

def hadamard_table(length):
    positions = jnp.arange(length, dtype=jnp.int32)
    common = jnp.bitwise_and(positions[:, None], positions[None, :])
    return parity_sign(common, length)

def hadamard_last(values):
    length = values.shape[-1]
    inner_len = min(128, length)
    outer_len = length // inner_len
    leading = values.shape[:-1]
    blocks = values.reshape(leading + (outer_len, inner_len))
    blocks = jnp.einsum('...ab,bc->...ac', blocks, hadamard_table(inner_len), precision=lax.Precision.HIGHEST)
    blocks = jnp.einsum('...ab,ac->...cb', blocks, hadamard_table(outer_len), precision=lax.Precision.HIGHEST)
    return blocks.reshape(values.shape) * (1.0 / math.sqrt(length))

def sign_table(packed):
    places = jnp.arange(16, dtype=jnp.int32)
    bit_values = jnp.bitwise_and(jnp.right_shift(packed[..., None], places), 1)
    return (1 - 2 * bit_values).astype(jnp.float32).reshape(packed.shape[:-1] + (packed.shape[-1] * 16,))

def reference(activations, out_grads, sign_bits, keep_cols, row_start, row_step, val_sketch):
    words = sign_bits.reshape(DI, N_EXAMPLE, N_SKETCH, WK // 16)
    words = jnp.transpose(words, (0, 2, 1, 3)).reshape(DI, DO // 16)
    sign_grid = sign_table(words)
    kept_count = keep_cols.shape[0]
    width_block = DO // kept_count
    columns = (jnp.arange(kept_count, dtype=jnp.int32) * width_block + keep_cols).astype(jnp.int32)
    strides = 2 * row_step + 1
    kept_rows = ((row_start[:, None] + jnp.arange(KR, dtype=jnp.int32)[None, :] * strides[:, None]) % DI).astype(jnp.int32)

    def one_example(example_pair):
        act_rows, grad_rows = example_pair
        gradient = lax.dot_general(act_rows, grad_rows, (((1,), (1,)), ((), ())), preferred_element_type=jnp.float32)
        transformed = hadamard_last(sign_grid * gradient)
        picked = jnp.take(transformed, columns, axis=1).T
        picked = hadamard_last(picked)
        return jnp.take_along_axis(picked, kept_rows, axis=1).reshape(-1)
    sketch = lax.map(one_example, (activations, out_grads))
    products = jnp.dot(sketch, val_sketch.T, precision=lax.Precision.HIGHEST)
    norm_sq = lax.optimization_barrier(jnp.sum(sketch * sketch, axis=1))
    return products / jnp.sqrt(norm_sq + 1e-06)[:, None]
```

```python
import functools
import math

import jax
import jax.numpy as jnp
from jax import lax
from jax.experimental import pallas as pl
from jax.experimental.pallas import tpu as pltpu
from jax.sharding import PartitionSpec as P

MESH = pl.DeviceIdType.MESH
F32 = jnp.float32
BF16 = jnp.bfloat16
I32 = jnp.int32
LANES = 128
BITS = 16
ROWS = 256
WIDE = 512


def log2(n):
    return n.bit_length() - 1


def sign_of(common):
    for shift in (16, 8, 4, 2, 1):
        common = jnp.bitwise_xor(common, jnp.right_shift(common, shift))
    return (1 - 2 * jnp.bitwise_and(common, 1)).astype(F32)


def iota(shape, axis):
    return lax.broadcasted_iota(I32, shape, axis)


def split(values):
    high = values.astype(BF16)
    return high, (values - high.astype(F32)).astype(BF16)


def place(s, c, k):
    return {"sketch": s, "context": c, "example": k}


def gradient_kernel(sizes, act, grads, words, columns, rows_in, val, part, rows_all, val_all,
                    a_buf, g_buf, gp, gt, table, perm, own_sem,
                    gz_send, gz_recv, az_send, az_recv, vz_send, vz_recv,
                    gx_send, gx_recv, ax_send, ax_recv, r_send, r_recv):
    S, C, E = sizes
    s, c, k = lax.axis_index("sketch"), lax.axis_index("context"), lax.axis_index("example")
    rp, gp_len = act.shape[1], grads.shape[1]
    ah, gh = rp // E, gp_len // C
    total_rows, total_cols = a_buf.shape[0], g_buf.shape[0]
    word_count = words.shape[1]

    barrier = pltpu.get_barrier_semaphore()
    away = [place(lax.rem(s + o, S), c, k) for o in range(1, S)]
    peers = [
        (lax.rem(c + m // E, C), lax.rem(k + m % E, E)) for m in range(1, C * E)
    ]
    for target in away + [place(s, pc, pk) for pc, pk in peers]:
        pl.semaphore_signal(barrier, inc=1, device_id=target, device_id_type=MESH)
    pl.semaphore_wait(barrier, S - 1 + C * E - 1)

    def remote(src, dst, send, recv, target):
        return pltpu.make_async_remote_copy(
            src_ref=src, dst_ref=dst, send_sem=send, recv_sem=recv,
            device_id=target, device_id_type=MESH)

    def g_rows(piece, part_at):
        return pl.ds(pl.multiple_of(piece * gp_len + part_at * gh, gh), gh)

    def a_rows(piece, part_at):
        return pl.ds(pl.multiple_of(piece * rp + part_at * ah, ah), ah)

    def g_send(o):
        t = lax.rem(s + o, S)
        return remote(grads.at[t, pl.ds(pl.multiple_of(c * gh, gh), gh)], g_buf.at[g_rows(s, c)],
                      gz_send.at[o], gz_recv.at[s], place(t, c, k))

    def a_send(o):
        t = lax.rem(s + o, S)
        return remote(act.at[t, pl.ds(pl.multiple_of(k * ah, ah), ah)], a_buf.at[a_rows(s, k)],
                      az_send.at[o], az_recv.at[s], place(t, c, k))

    def v_send(o):
        t = lax.rem(s + o, S)
        return remote(val, val_all.at[s], vz_send.at[o], vz_recv.at[s], place(t, c, k))

    def g_pass(piece, m):
        return remote(g_buf.at[g_rows(piece, c)], g_buf.at[g_rows(piece, c)],
                      gx_send.at[piece, m], gx_recv.at[piece, c], place(s, lax.rem(c + m, C), k))

    def a_pass(piece, m):
        return remote(a_buf.at[a_rows(piece, k)], a_buf.at[a_rows(piece, k)],
                      ax_send.at[piece, m], ax_recv.at[piece, k], place(s, c, lax.rem(k + m, E)))

    def arrived(ref, sem):
        pltpu.make_async_copy(ref, ref, sem).wait()

    me = c * E + k
    started = []

    def start(copy):
        copy.start()
        started.append(copy)

    for o in range(1, S):
        start(g_send(o))
    own_g = pltpu.make_async_copy(
        grads.at[s], g_buf.at[pl.ds(pl.multiple_of(s * gp_len, gp_len), gp_len)], own_sem.at[0])
    own_a = pltpu.make_async_copy(
        act.at[s], a_buf.at[pl.ds(pl.multiple_of(s * rp, rp), rp)], own_sem.at[1])
    own_v = pltpu.make_async_copy(val, val_all.at[s], own_sem.at[2])
    own_g.start()
    own_a.start()
    for m, (pc, pk) in enumerate(peers):
        start(remote(rows_in, rows_all.at[me], r_send.at[m], r_recv.at[me], place(s, pc, pk)))
    rows_all[pl.ds(me, 1)] = rows_in[...][None]

    kept = columns[...]
    for b in range(BITS):
        local = iota((word_count, LANES), 0) * BITS + b
        shift = log2(gp_len)
        full = ((jnp.right_shift(local, shift) * E + k) * gp_len
                + jnp.bitwise_and(local, gp_len - 1))
        table[b * word_count:(b + 1) * word_count, :] = sign_of(
            jnp.bitwise_and(full, kept)).astype(BF16)

    block = perm.shape[0]
    block_words = block // BITS
    blocks = total_cols // block
    row_at, col_at = iota((block, block), 0), iota((block, block), 1)
    source = (jnp.bitwise_and(row_at, block_words - 1) * BITS
              + jnp.right_shift(row_at, log2(block_words)))
    perm[...] = jnp.where(col_at == source, 1.0, 0.0).astype(BF16)

    def permute(at):
        rows = g_buf[pl.ds(pl.multiple_of(at * block, block), block), :]
        moved = jnp.dot(perm[...], rows, preferred_element_type=F32).astype(BF16)
        for b in range(BITS):
            gp[pl.ds(pl.multiple_of(b * word_count + at * block_words, block_words),
                     block_words), :] = moved[b * block_words:(b + 1) * block_words]

    for o in range(1, S):
        piece = lax.rem(s - o + S, S)
        arrived(g_buf.at[g_rows(piece, c)], gz_recv.at[piece])
        start(a_send(o))
        for m in range(1, C):
            start(g_pass(piece, m))
    own_v.start()
    for o in range(1, S):
        start(v_send(o))
    own_g.wait()
    pieces_in_block = max(1, block // gp_len)
    first = s // pieces_in_block
    if blocks * pieces_in_block == S and pieces_in_block == 1:
        permute(s)
    for o in range(1, S):
        piece = lax.rem(s - o + S, S)
        for m in range(1, C):
            other = lax.rem(c + m, C)
            arrived(g_buf.at[g_rows(piece, other)], gx_recv.at[piece, other])
        if blocks * pieces_in_block == S and pieces_in_block == 1:
            permute(piece)
    if not (blocks * pieces_in_block == S and pieces_in_block == 1):
        lax.fori_loop(0, blocks, lambda at, _: (permute(at), 0)[1], 0)
    wide = min(WIDE, total_cols)
    for at in range(total_cols // wide):
        gt[:, at * wide:(at + 1) * wide] = gp[at * wide:(at + 1) * wide, :].T

    row_block = min(ROWS, rp)

    def score_rows(row):
        here = pl.ds(pl.multiple_of(row, row_block), row_block)
        a = a_buf[here, :]
        w = words[here, :]
        total = jnp.zeros((row_block, LANES), F32)
        for at in range(total_cols // wide):
            grad = jnp.dot(a, gt[:, at * wide:(at + 1) * wide], preferred_element_type=F32)
            signed = []
            for bb in range(wide // word_count):
                bit = 1 << (at * (wide // word_count) + bb)
                one = grad[:, bb * word_count:(bb + 1) * word_count]
                signed.append(jnp.where(jnp.bitwise_and(w, bit) != 0, -one, one))
            high, low = split(jnp.concatenate(signed, axis=1))
            side = table[at * wide:(at + 1) * wide, :]
            total = total + jnp.dot(high, side, preferred_element_type=F32)
            total = total + jnp.dot(low, side, preferred_element_type=F32)
        part[here, :] = total

    def score_piece(piece):
        lax.fori_loop(
            0, rp // row_block,
            lambda at, _: (score_rows(piece * rp + at * row_block), 0)[1], 0)

    own_a.wait()
    score_piece(s)
    for o in range(1, S):
        piece = lax.rem(s - o + S, S)
        arrived(a_buf.at[a_rows(piece, k)], az_recv.at[piece])
        for m in range(1, E):
            start(a_pass(piece, m))
        for m in range(1, E):
            other = lax.rem(k + m, E)
            arrived(a_buf.at[a_rows(piece, other)], ax_recv.at[piece, other])
        score_piece(piece)
    for pc, pk in peers:
        arrived(rows_all.at[pc * E + pk], r_recv.at[pc * E + pk])
    own_v.wait()
    for o in range(1, S):
        piece = lax.rem(s - o + S, S)
        arrived(val_all.at[piece], vz_recv.at[piece])
    for copy in started:
        copy.wait_send()


def sketch_kernel(sizes, scale, kr, part, rows_all, out, turned, plain):
    S, C, E = sizes
    c = lax.axis_index("context")
    total_rows = part.shape[0]
    rp = total_rows // S
    in_width = total_rows * C
    q_count = C * E
    block = min(ROWS, total_rows)
    table = sign_of(
        jnp.bitwise_and(iota((block, block), 0), iota((block, block), 1))).astype(BF16)
    mixed = []
    for at in range(total_rows // block):
        both = jnp.concatenate(split(part[at * block:(at + 1) * block, :]), axis=1)
        got = jnp.dot(table, both, preferred_element_type=F32)
        mixed.append(got[:, :LANES] + got[:, LANES:])
    step = 1
    while step < len(mixed):
        nxt = list(mixed)
        for at in range(len(mixed)):
            if at & step == 0:
                nxt[at] = mixed[at] + mixed[at + step]
                nxt[at + step] = mixed[at] - mixed[at + step]
        mixed = nxt
        step *= 2
    for at, values in enumerate(mixed):
        for b in range(0, block, LANES):
            turned[at * block + b:at * block + b + LANES, :] = values[b:b + LANES, :].T

    lane = iota((1, LANES), 1)
    per = LANES // q_count
    begin = jnp.zeros((1, LANES), I32)
    half = jnp.zeros((1, LANES), I32)
    for q in range(q_count):
        mine = jnp.right_shift(lane, log2(per)) == q
        begin = jnp.where(mine, rows_all[q, 0:1, :], begin)
        half = jnp.where(mine, rows_all[q, 1:2, :], half)
    fold = LANES // kr
    high_rows = LANES // fold
    shape = (high_rows, LANES)
    wide_lane = iota(shape, 1)
    at_i = jnp.bitwise_and(wide_lane, kr - 1)
    group = jnp.right_shift(wide_lane, log2(kr))

    def down(vector):
        plain[...] = jnp.broadcast_to(vector, (LANES, LANES)).T
        got = plain[pl.ds(0, high_rows, stride=fold), :]
        for f in range(1, fold):
            got = jnp.where(group == f, plain[pl.ds(f, high_rows, stride=fold), :], got)
        return got

    row = jnp.bitwise_and(down(begin) + at_i * (2 * down(half) + 1), in_width - 1)
    piece_bits, context_bits = log2(rp), log2(C)
    sign = sign_of(jnp.bitwise_and(jnp.bitwise_and(jnp.right_shift(row, piece_bits), C - 1), c))
    local = (jnp.left_shift(jnp.right_shift(row, piece_bits + context_bits), piece_bits)
             + jnp.bitwise_and(row, rp - 1))
    in_block = jnp.bitwise_and(local, LANES - 1)
    which = jnp.right_shift(local, log2(LANES))
    picked = jnp.zeros(shape, F32)
    for at in range(total_rows // LANES):
        found = None
        for f in range(fold):
            values = turned[pl.ds(at * LANES + f, high_rows, stride=fold), :]
            got = jnp.take_along_axis(values, in_block, axis=1, mode="promise_in_bounds")
            found = got if found is None else jnp.where(group == f, got, found)
        picked = jnp.where(which == at, found, picked)
    out[...] = picked * sign * scale


def score_kernel(sizes, sketch, val, out, parts, sums, send, recv, send2, recv2):
    S, C, E = sizes
    s, c, k = lax.axis_index("sketch"), lax.axis_index("context"), lax.axis_index("example")
    q_count = C * E
    per = sketch.shape[0] // q_count
    nv = val.shape[0]
    me = c * E + k
    barrier = pltpu.get_barrier_semaphore()
    peers = [
        (lax.rem(c + m // E, C), lax.rem(k + m % E, E)) for m in range(1, q_count)
    ]
    for pc, pk in peers:
        pl.semaphore_signal(barrier, inc=1, device_id=place(s, pc, pk), device_id_type=MESH)
    pl.semaphore_wait(barrier, q_count - 1)

    copies = []
    for m, (pc, pk) in enumerate(peers):
        rows = pl.ds(pl.multiple_of((pc * E + pk) * per, per), per)
        copies.append(pltpu.make_async_remote_copy(
            src_ref=sketch.at[rows], dst_ref=parts.at[me], send_sem=send.at[m],
            recv_sem=recv.at[me], device_id=place(s, pc, pk), device_id_type=MESH))
        copies[-1].start()
    parts[pl.ds(me, 1)] = sketch[pl.ds(pl.multiple_of(me * per, per), per), :][None]
    for pc, pk in peers:
        ref = parts.at[pc * E + pk]
        pltpu.make_async_copy(ref, ref, recv.at[pc * E + pk]).wait()
    own = parts[0]
    for q in range(1, q_count):
        own = own + parts[q]
    total = jnp.zeros((nv, LANES), F32)
    for r in range(per):
        total = total + val[:, r * LANES:(r + 1) * LANES] * own[r:r + 1, :]
    squares = jnp.sum(own * own, axis=0, keepdims=True)
    tall = jnp.concatenate(
        [total, squares, jnp.zeros((LANES - nv - 1, LANES), F32)], axis=0)
    mine = jnp.sum(tall.T, axis=0, keepdims=True)
    sums[pl.ds(me, 1)] = jnp.broadcast_to(mine, (8, LANES))[None]
    for m, (pc, pk) in enumerate(peers):
        copies.append(pltpu.make_async_remote_copy(
            src_ref=sums.at[me], dst_ref=sums.at[me], send_sem=send2.at[m],
            recv_sem=recv2.at[me], device_id=place(s, pc, pk), device_id_type=MESH))
        copies[-1].start()
    for pc, pk in peers:
        ref = sums.at[pc * E + pk]
        pltpu.make_async_copy(ref, ref, recv2.at[pc * E + pk]).wait()
    all_sums = sums[0]
    for q in range(1, q_count):
        all_sums = all_sums + sums[q]
    out[...] = all_sums[0:1, :nv] / jnp.sqrt(all_sums[0:1, nv:nv + 1] + 1e-06)
    for copy in copies:
        copy.wait_send()


def body(activations, out_grads, sign_bits, keep_cols, row_start, row_step, val_sketch):
    S, C, E = lax.axis_size("sketch"), lax.axis_size("context"), lax.axis_size("example")
    sizes = (S, C, E)
    rp, tokens = activations.shape[1:]
    gp_len = out_grads.shape[1]
    local_rows, local_cols = S * rp, S * gp_len
    in_width, out_width = local_rows * C, local_cols * E
    kept = keep_cols.shape[0]
    q_count = C * E
    keep = val_sketch.shape[1] * q_count
    kr = keep // kept
    nv = val_sketch.shape[0] * S
    words = sign_bits.reshape(local_rows, -1)
    columns = (jnp.arange(kept, dtype=I32) * (out_width // kept) + keep_cols)[None, :]
    rows_in = jnp.concatenate(
        [jnp.tile(row_start, q_count)[None], jnp.tile(row_step, q_count)[None],
         jnp.zeros((6, kept), I32)], axis=0)
    vmem = pl.BlockSpec(memory_space=pltpu.VMEM)
    hbm = pl.BlockSpec(memory_space=pl.ANY)
    dma = pltpu.SemaphoreType.DMA
    block = min(WIDE, local_cols)
    part, rows_all, val_all = pl.pallas_call(
        functools.partial(gradient_kernel, sizes),
        out_shape=(
            jax.ShapeDtypeStruct((local_rows, kept), F32),
            jax.ShapeDtypeStruct((q_count, 8, kept), I32),
            jax.ShapeDtypeStruct((S,) + val_sketch.shape, F32),
        ),
        in_specs=[hbm, hbm, vmem, vmem, vmem, hbm],
        out_specs=(vmem, vmem, hbm),
        scratch_shapes=[
            pltpu.VMEM((local_rows, tokens), BF16),
            pltpu.VMEM((local_cols, tokens), BF16),
            pltpu.VMEM((local_cols, tokens), BF16),
            pltpu.VMEM((tokens, local_cols), BF16),
            pltpu.VMEM((local_cols, kept), BF16),
            pltpu.VMEM((block, block), BF16),
            dma((3,)),
            dma((S,)), dma((S,)), dma((S,)), dma((S,)), dma((S,)), dma((S,)),
            dma((S, C)), dma((S, C)), dma((S, E)), dma((S, E)),
            dma((q_count,)), dma((q_count,)),
        ],
        compiler_params=pltpu.CompilerParams(
            collective_id=0, has_side_effects=True, vmem_limit_bytes=44 * 2**20),
        cost_estimate=pl.CostEstimate(
            flops=2 * local_rows * local_cols * (tokens + 2 * kept),
            bytes_accessed=2 * (local_rows + local_cols) * tokens, transcendentals=0),
        name="gradient",
    )(activations, out_grads, words, columns, rows_in, val_sketch)
    sketch = pl.pallas_call(
        functools.partial(
            sketch_kernel, sizes, 1.0 / (math.sqrt(in_width) * math.sqrt(out_width)), kr),
        out_shape=jax.ShapeDtypeStruct((keep // LANES, LANES), F32),
        in_specs=[vmem, vmem],
        out_specs=vmem,
        scratch_shapes=[
            pltpu.VMEM((local_rows, LANES), F32),
            pltpu.VMEM((LANES, LANES), I32),
        ],
        compiler_params=pltpu.CompilerParams(vmem_limit_bytes=32 * 2**20),
        name="sketch",
    )(part, rows_all)
    return pl.pallas_call(
        functools.partial(score_kernel, sizes),
        out_shape=jax.ShapeDtypeStruct((1, nv), F32),
        in_specs=[vmem, vmem],
        out_specs=vmem,
        scratch_shapes=[
            pltpu.VMEM((q_count, keep // LANES // q_count, LANES), F32),
            pltpu.VMEM((q_count, 8, LANES), F32),
            dma((q_count,)), dma((q_count,)), dma((q_count,)), dma((q_count,)),
        ],
        compiler_params=pltpu.CompilerParams(
            collective_id=1, has_side_effects=True, vmem_limit_bytes=32 * 2**20),
        name="score",
    )(sketch, val_all.reshape(nv, -1))


def solution(mesh):
    placed = (
        P("groups", ("sketch", "context"), None),
        P("groups", ("sketch", "example"), None),
        P(None, "context", None, "example", None),
        P(),
        P(("context", "example")),
        P(("context", "example")),
        P("sketch", ("context", "example")),
    )
    return jax.shard_map(
        body, mesh=mesh, in_specs=placed, out_specs=P(("groups", "sketch"), None), check_vma=False
    )
```

```python
import functools
import math

import jax
import jax.numpy as jnp
from jax import lax
from jax.experimental import pallas as pl
from jax.experimental.pallas import tpu as pltpu
from jax.sharding import PartitionSpec as P

MESH = pl.DeviceIdType.MESH
F32 = jnp.float32
BF16 = jnp.bfloat16
I32 = jnp.int32
LANES = 128
BITS = 16
ROWS = 256
WIDE = 512


def log2(n):
    return n.bit_length() - 1


def sign_of(common):
    for shift in (16, 8, 4, 2, 1):
        common = jnp.bitwise_xor(common, jnp.right_shift(common, shift))
    return (1 - 2 * jnp.bitwise_and(common, 1)).astype(F32)


def iota(shape, axis):
    return lax.broadcasted_iota(I32, shape, axis)


def split(values):
    high = values.astype(BF16)
    return high, (values - high.astype(F32)).astype(BF16)


def place(s, c, k):
    return {"sketch": s, "context": c, "example": k}


def each(count, step):
    if count <= 32:
        for at in range(1, count):
            step(at)
    else:
        lax.fori_loop(1, count, lambda at, _: (step(at), 0)[1], 0)


def kernel(sizes, scale, kr, act, grads, words_in, columns_in, begin_in, half_in, val_in, out,
           a_buf, g_buf, gp, gt, table, perm, hada, words, columns, begins, halves, val,
           part, turned, plain, ring, sketch, parts, sums,
           own_sem, gz_send, gz_recv, az_send, az_recv, gx_send, gx_recv, ax_send, ax_recv,
           r_send, r_recv, p_send, p_recv, s_send, s_recv):
    S, C, E = sizes
    Q = C * E
    s, c, k = lax.axis_index("sketch"), lax.axis_index("context"), lax.axis_index("example")
    me = c * E + k
    rp, gp_len = act.shape[1], grads.shape[1]
    gh = gp_len // C
    row_block = min(ROWS, rp)
    halves_of = rp // row_block
    ah = row_block // E
    total_rows, total_cols = a_buf.shape[0], g_buf.shape[0]
    in_width, out_width = total_rows * C, total_cols * E
    word_count = words.shape[1]
    kept = columns.shape[1]

    def member(m):
        t = lax.rem(s + lax.div(m, Q), S)
        q = lax.rem(me + lax.rem(m, Q), Q)
        return t, q

    def spot(t, q):
        return place(t, lax.div(q, E), lax.rem(q, E))

    barrier = pltpu.get_barrier_semaphore()

    def greet(m):
        pl.semaphore_signal(barrier, inc=1, device_id=spot(*member(jnp.int32(m))),
                            device_id_type=MESH)

    local = [
        pltpu.make_async_copy(src, dst, own_sem.at[at]) for at, (src, dst) in enumerate((
            (begin_in, begins), (half_in, halves), (columns_in, columns),
            (grads.at[s], g_buf.at[pl.ds(pl.multiple_of(s * gp_len, gp_len), gp_len)]),
            (act.at[s], a_buf.at[pl.ds(pl.multiple_of(s * rp, rp), rp)]),
            (words_in, words), (val_in, val)))
    ]
    each(S * Q, greet)
    for copy in local[:3]:
        copy.start()
    pl.semaphore_wait(barrier, S * Q - 1)

    def remote(src, dst, send, recv, target):
        return pltpu.make_async_remote_copy(
            src_ref=src, dst_ref=dst, send_sem=send, recv_sem=recv,
            device_id=target, device_id_type=MESH)

    def g_rows(piece, part_at):
        return pl.ds(pl.multiple_of(piece * gp_len + part_at * gh, gh), gh)

    def a_rows(piece, h, part_at):
        return pl.ds(pl.multiple_of(piece * rp + h * row_block + part_at * ah, ah), ah)

    def g_send(o):
        t = lax.rem(s + o, S)
        return remote(grads.at[t, pl.ds(pl.multiple_of(c * gh, gh), gh)], g_buf.at[g_rows(s, c)],
                      gz_send.at[o], gz_recv.at[s], place(t, c, k))

    def a_send(o, h):
        t = lax.rem(s + o, S)
        return remote(act.at[t, pl.ds(pl.multiple_of(h * row_block + k * ah, ah), ah)],
                      a_buf.at[a_rows(s, h, k)], az_send.at[o, h], az_recv.at[s, h],
                      place(t, c, k))

    def g_pass(piece, m):
        return remote(g_buf.at[g_rows(piece, c)], g_buf.at[g_rows(piece, c)],
                      gx_send.at[piece, m], gx_recv.at[piece, c], place(s, lax.rem(c + m, C), k))

    def a_pass(piece, h, m):
        rows = a_rows(piece, h, k)
        return remote(a_buf.at[rows], a_buf.at[rows], ax_send.at[piece, h, m],
                      ax_recv.at[piece, h, k], place(s, c, lax.rem(k + m, E)))

    def arrived(ref, sem):
        pltpu.make_async_copy(ref, ref, sem).wait()

    started = []

    def start(copy):
        copy.start()
        started.append(copy)

    for o in range(1, S):
        start(g_send(o))
    for copy in local[3:]:
        copy.start()

    for copy in local[:2]:
        copy.wait()
    per_q = kept // Q
    ring[pl.ds(me, 1)] = jnp.zeros((1, 8, kept), I32)
    for q in range(Q):
        ring[me, 0:1, q * per_q:(q + 1) * per_q] = begins[...]
        ring[me, 1:2, q * per_q:(q + 1) * per_q] = halves[...]
    for m in range(1, Q):
        q = lax.rem(me + m, Q)
        start(remote(ring.at[me], ring.at[me], r_send.at[m], r_recv.at[me], spot(s, q)))

    local[2].wait()
    width = out_width // kept
    kept_cols = columns[...] + iota((1, kept), 1) * width
    for b in range(BITS):
        at = iota((word_count, kept), 0) * BITS + b
        full = ((jnp.right_shift(at, log2(gp_len)) * E + k) * gp_len
                + jnp.bitwise_and(at, gp_len - 1))
        table[b * word_count:(b + 1) * word_count, :] = sign_of(
            jnp.bitwise_and(full, kept_cols)).astype(BF16)
    hada[...] = sign_of(jnp.bitwise_and(
        iota((row_block, row_block), 0), iota((row_block, row_block), 1))).astype(BF16)

    block = perm.shape[0]
    block_words = block // BITS
    blocks = total_cols // block
    row_at, col_at = iota((block, block), 0), iota((block, block), 1)
    source = (jnp.bitwise_and(row_at, block_words - 1) * BITS
              + jnp.right_shift(row_at, log2(block_words)))
    perm[...] = jnp.where(col_at == source, 1.0, 0.0).astype(BF16)

    def permute(at):
        rows = g_buf[pl.ds(pl.multiple_of(at * block, block), block), :]
        moved = jnp.dot(perm[...], rows, preferred_element_type=F32).astype(BF16)
        for b in range(BITS):
            gp[pl.ds(pl.multiple_of(b * word_count + at * block_words, block_words),
                     block_words), :] = moved[b * block_words:(b + 1) * block_words]

    for o in range(1, S):
        piece = lax.rem(s - o + S, S)
        arrived(g_buf.at[g_rows(piece, c)], gz_recv.at[piece])
        for h in range(halves_of):
            start(a_send(o, h))
        for m in range(1, C):
            start(g_pass(piece, m))
    local[3].wait()
    piece_blocks = block == gp_len
    if piece_blocks:
        permute(s)
    for o in range(1, S):
        piece = lax.rem(s - o + S, S)
        for m in range(1, C):
            other = lax.rem(c + m, C)
            arrived(g_buf.at[g_rows(piece, other)], gx_recv.at[piece, other])
        if piece_blocks:
            permute(piece)
    if not piece_blocks:
        lax.fori_loop(0, blocks, lambda at, _: (permute(at), 0)[1], 0)
    wide = min(WIDE, total_cols)
    for at in range(total_cols // wide):
        gt[:, at * wide:(at + 1) * wide] = gp[at * wide:(at + 1) * wide, :].T

    def score_rows(row):
        here = pl.ds(pl.multiple_of(row, row_block), row_block)
        a = a_buf[here, :]
        w = words[here, :]
        total = jnp.zeros((row_block, kept), F32)
        for at in range(total_cols // wide):
            grad = jnp.dot(a, gt[:, at * wide:(at + 1) * wide], preferred_element_type=F32)
            signed = []
            for bb in range(wide // word_count):
                bit = 1 << (at * (wide // word_count) + bb)
                one = grad[:, bb * word_count:(bb + 1) * word_count]
                signed.append(jnp.where(jnp.bitwise_and(w, bit) != 0, -one, one))
            high, low = split(jnp.concatenate(signed, axis=1))
            side = table[at * wide:(at + 1) * wide, :]
            total = total + jnp.dot(high, side, preferred_element_type=F32)
            total = total + jnp.dot(low, side, preferred_element_type=F32)
        got = jnp.dot(hada[...], jnp.concatenate(split(total), axis=1),
                      preferred_element_type=F32)
        part[here, :] = got[:, :kept] + got[:, kept:]

    local[4].wait()
    local[5].wait()
    lax.fori_loop(0, halves_of, lambda h, _: (score_rows(s * rp + h * row_block), 0)[1], 0)
    for o in range(1, S):
        piece = lax.rem(s - o + S, S)
        for h in range(halves_of):
            arrived(a_buf.at[a_rows(piece, h, k)], az_recv.at[piece, h])
            for m in range(1, E):
                start(a_pass(piece, h, m))
            for m in range(1, E):
                other = lax.rem(k + m, E)
                arrived(a_buf.at[a_rows(piece, h, other)], ax_recv.at[piece, h, other])
            score_rows(piece * rp + h * row_block)

    mixed = [part[at:at + row_block, :] for at in range(0, total_rows, row_block)]
    step = 1
    while step < len(mixed):
        nxt = list(mixed)
        for at in range(len(mixed)):
            if at & step == 0:
                nxt[at] = mixed[at] + mixed[at + step]
                nxt[at + step] = mixed[at] - mixed[at + step]
        mixed = nxt
        step *= 2
    whole = mixed if row_block >= LANES else [
        jnp.concatenate(mixed[at:at + LANES // row_block], axis=0)
        for at in range(0, len(mixed), LANES // row_block)]
    turned_rows = 0
    for values in whole:
        for b in range(0, values.shape[0], LANES):
            turned[turned_rows:turned_rows + LANES, :] = values[b:b + LANES, :].T
            turned_rows += LANES

    for m in range(1, Q):
        q = lax.rem(me + m, Q)
        arrived(ring.at[q], r_recv.at[q])
    lane = iota((1, kept), 1)
    begin = jnp.zeros((1, kept), I32)
    half = jnp.zeros((1, kept), I32)
    for q in range(Q):
        mine = jnp.right_shift(lane, log2(per_q)) == q
        begin = jnp.where(mine, ring[q, 0:1, :], begin)
        half = jnp.where(mine, ring[q, 1:2, :], half)
    fold = LANES // kr
    high_rows = kept // fold
    shape = (high_rows, LANES)
    wide_lane = iota(shape, 1)
    at_i = jnp.bitwise_and(wide_lane, kr - 1)
    group = jnp.right_shift(wide_lane, log2(kr))

    def down(vector):
        plain[...] = jnp.broadcast_to(vector, (kept, kept)).T
        got = plain[pl.ds(0, high_rows, stride=fold), :]
        for f in range(1, fold):
            got = jnp.where(group == f, plain[pl.ds(f, high_rows, stride=fold), :], got)
        return got

    row = jnp.bitwise_and(down(begin) + at_i * (2 * down(half) + 1), in_width - 1)
    piece_bits, context_bits = log2(rp), log2(C)
    sign = sign_of(jnp.bitwise_and(jnp.bitwise_and(jnp.right_shift(row, piece_bits), C - 1), c))
    held = (jnp.left_shift(jnp.right_shift(row, piece_bits + context_bits), piece_bits)
            + jnp.bitwise_and(row, rp - 1))
    in_block = jnp.bitwise_and(held, LANES - 1)
    which = jnp.right_shift(held, log2(LANES))
    picked = jnp.zeros(shape, F32)
    for at in range(total_rows // LANES):
        found = None
        for f in range(fold):
            values = turned[pl.ds(at * LANES + f, high_rows, stride=fold), :]
            got = jnp.take_along_axis(values, in_block, axis=1, mode="promise_in_bounds")
            found = got if found is None else jnp.where(group == f, got, found)
        picked = jnp.where(which == at, found, picked)
    sketch[...] = picked * sign * scale

    per = high_rows // Q
    mine_at = s * Q + me

    def q_rows(q):
        return pl.ds(pl.multiple_of(q * per, per), per)

    def p_copy(m):
        t, q = member(jnp.int32(m))
        return remote(sketch.at[q_rows(q)], parts.at[mine_at], p_send.at[m], p_recv.at[mine_at],
                      spot(t, q))

    each(S * Q, lambda m: p_copy(m).start())
    parts[pl.ds(mine_at, 1)] = sketch[q_rows(me), :][None]
    local[6].wait()

    def p_arrived(m):
        t, q = member(jnp.int32(m))
        arrived(parts.at[t * Q + q], p_recv.at[t * Q + q])

    each(S * Q, p_arrived)
    nvl = val.shape[0]
    nv = nvl * S
    out_lane = iota((1, LANES), 1)

    def products(e):
        own = parts[e * Q]
        for q in range(1, Q):
            own = own + parts[e * Q + q]
        total = jnp.zeros((nvl, LANES), F32)
        for r in range(per):
            total = total + val[:, r * LANES:(r + 1) * LANES] * own[r:r + 1, :]
        squares = jnp.sum(own * own, axis=0, keepdims=True)
        tall = jnp.concatenate(
            [total, squares, jnp.zeros((LANES - nvl - 1, LANES), F32)], axis=0)
        line = jnp.sum(tall.T, axis=0, keepdims=True)
        norm = jnp.sum(squares, axis=1, keepdims=True)
        mine = pltpu.roll(jnp.where(out_lane < nvl, line, 0.0), s * nvl, axis=1)
        mine = jnp.where(out_lane == nv, norm * (s == 0).astype(F32), mine)
        return jnp.broadcast_to(mine, (8, LANES))

    answers = part

    def e_rows(e):
        return pl.ds(pl.multiple_of(e * 8, 8), 8)

    if S <= 16:
        for e in range(S):
            answers[e * 8:(e + 1) * 8, :] = products(e)
    else:
        def put(e, carry):
            answers[e_rows(e), :] = products(e)
            return carry
        lax.fori_loop(0, S, put, 0)

    def s_copy(m):
        t, q = member(jnp.int32(m))
        return remote(answers.at[e_rows(t)], sums.at[mine_at], s_send.at[m], s_recv.at[mine_at],
                      spot(t, q))

    each(S * Q, lambda m: s_copy(m).start())
    sums[pl.ds(mine_at, 1)] = answers[e_rows(s), :][None]

    def s_arrived(m):
        t, q = member(jnp.int32(m))
        arrived(sums.at[t * Q + q], s_recv.at[t * Q + q])

    each(S * Q, s_arrived)
    all_sums = sums[0]
    for at in range(1, S * Q):
        all_sums = all_sums + sums[at]
    out[...] = all_sums[0:1, :nv] / jnp.sqrt(all_sums[0:1, nv:nv + 1] + 1e-06)
    for copy in started:
        copy.wait_send()
    each(S * Q, lambda m: p_copy(m).wait_send())
    each(S * Q, lambda m: s_copy(m).wait_send())


def body(activations, out_grads, sign_bits, keep_cols, row_start, row_step, val_sketch):
    S, C, E = lax.axis_size("sketch"), lax.axis_size("context"), lax.axis_size("example")
    Q = C * E
    rp, tokens = activations.shape[1:]
    gp_len = out_grads.shape[1]
    local_rows, local_cols = S * rp, S * gp_len
    in_width, out_width = local_rows * C, local_cols * E
    kept = keep_cols.shape[0]
    keep = val_sketch.shape[1] * Q
    kr = keep // kept
    nv = val_sketch.shape[0] * S
    words = sign_bits.reshape(local_rows, -1)
    row_block = min(ROWS, rp)
    halves = rp // row_block
    hbm = pl.BlockSpec(memory_space=pl.ANY)
    dma = pltpu.SemaphoreType.DMA
    block = min(WIDE, local_cols)
    return pl.pallas_call(
        functools.partial(
            kernel, (S, C, E), 1.0 / (math.sqrt(in_width) * math.sqrt(out_width)), kr),
        out_shape=jax.ShapeDtypeStruct((1, nv), F32),
        in_specs=[hbm] * 7,
        out_specs=pl.BlockSpec(memory_space=pltpu.VMEM),
        scratch_shapes=[
            pltpu.VMEM((local_rows, tokens), BF16),
            pltpu.VMEM((local_cols, tokens), BF16),
            pltpu.VMEM((local_cols, tokens), BF16),
            pltpu.VMEM((tokens, local_cols), BF16),
            pltpu.VMEM((local_cols, kept), BF16),
            pltpu.VMEM((block, block), BF16),
            pltpu.VMEM((row_block, row_block), BF16),
            pltpu.VMEM(words.shape, I32),
            pltpu.VMEM((1, kept), I32),
            pltpu.VMEM((1, kept // Q), I32),
            pltpu.VMEM((1, kept // Q), I32),
            pltpu.VMEM(val_sketch.shape, F32),
            pltpu.VMEM((local_rows, kept), F32),
            pltpu.VMEM((local_rows, LANES), F32),
            pltpu.VMEM((kept, kept), I32),
            pltpu.VMEM((Q, 8, kept), I32),
            pltpu.VMEM((keep // LANES, LANES), F32),
            pltpu.VMEM((S * Q, keep // LANES // Q, LANES), F32),
            pltpu.VMEM((S * Q, 8, LANES), F32),
            dma((7,)),
            dma((S,)), dma((S,)), dma((S, halves)), dma((S, halves)),
            dma((S, C)), dma((S, C)), dma((S, halves, E)), dma((S, halves, E)),
            dma((Q,)), dma((Q,)),
            dma((S * Q,)), dma((S * Q,)), dma((S * Q,)), dma((S * Q,)),
        ],
        compiler_params=pltpu.CompilerParams(
            collective_id=0, has_side_effects=True, vmem_limit_bytes=60 * 2**20),
        cost_estimate=pl.CostEstimate(
            flops=2 * local_rows * local_cols * (tokens + 2 * kept),
            bytes_accessed=2 * (local_rows + local_cols) * tokens, transcendentals=0),
        name="scores",
    )(activations, out_grads, words, keep_cols[None], row_start[None], row_step[None], val_sketch)


def solution(mesh):
    placed = (
        P("groups", ("sketch", "context"), None),
        P("groups", ("sketch", "example"), None),
        P(None, "context", None, "example", None),
        P(),
        P(("context", "example")),
        P(("context", "example")),
        P("sketch", ("context", "example")),
    )
    return jax.shard_map(
        body, mesh=mesh, in_specs=placed, out_specs=P(("groups", "sketch"), None), check_vma=False
    )
```

```python
import functools
import math

import jax
import jax.numpy as jnp
from jax import lax
from jax.experimental import pallas as pl
from jax.experimental.pallas import tpu as pltpu
from jax.sharding import PartitionSpec as P

MESH = pl.DeviceIdType.MESH
F32 = jnp.float32
BF16 = jnp.bfloat16
I32 = jnp.int32
LANES = 128
BITS = 16
ROWS = 256
WIDE = 512


def log2(n):
    return n.bit_length() - 1


def sign_of(common):
    for shift in (16, 8, 4, 2, 1):
        common = jnp.bitwise_xor(common, jnp.right_shift(common, shift))
    return (1 - 2 * jnp.bitwise_and(common, 1)).astype(F32)


def iota(shape, axis):
    return lax.broadcasted_iota(I32, shape, axis)


def split(values):
    high = values.astype(BF16)
    return high, (values - high.astype(F32)).astype(BF16)


def place(s, c, k):
    return {"sketch": s, "context": c, "example": k}


def each(count, step):
    lax.fori_loop(1, count, lambda at, _: (step(at), 0)[1], 0)


def kernel(sizes, scale, kr, act, grads, words_in, columns_in, begin_in, half_in, val_in, out,
           a_buf, g_buf, gp, gt, table, perm, hada, words, columns, begins, halves, val,
           part, turned, plain, ring, sketch, parts, sums,
           own_sem, gz_send, gz_recv, az_send, az_recv, gx_send, gx_recv, ax_send, ax_recv,
           r_send, r_recv, p_send, p_recv, s_send, s_recv):
    S, C, E = sizes
    Q = C * E
    s, c, k = lax.axis_index("sketch"), lax.axis_index("context"), lax.axis_index("example")
    me = c * E + k
    rp, gp_len = act.shape[1], grads.shape[1]
    gh = gp_len // C
    ah = rp // E
    row_block = min(ROWS, ah)
    total_rows, total_cols = a_buf.shape[0], g_buf.shape[0]
    in_width, out_width = total_rows * C, total_cols * E
    word_count = words.shape[1]
    kept = columns.shape[1]

    def member(m):
        t = lax.rem(s + lax.div(m, Q), S)
        q = lax.rem(me + lax.rem(m, Q), Q)
        return t, q

    def spot(t, q):
        return place(t, lax.div(q, E), lax.rem(q, E))

    barrier = pltpu.get_barrier_semaphore()

    def greet(m):
        pl.semaphore_signal(barrier, inc=1, device_id=spot(*member(jnp.int32(m))),
                            device_id_type=MESH)

    local = [
        pltpu.make_async_copy(src, dst, own_sem.at[at]) for at, (src, dst) in enumerate((
            (begin_in, begins), (half_in, halves), (columns_in, columns),
            (grads.at[s], g_buf.at[pl.ds(pl.multiple_of(s * gp_len, gp_len), gp_len)]),
            (act.at[s], a_buf.at[pl.ds(pl.multiple_of(s * rp, rp), rp)]),
            (words_in, words), (val_in, val)))
    ]
    each(S * Q, greet)
    for copy in local[:3]:
        copy.start()
    pl.semaphore_wait(barrier, S * Q - 1)

    def remote(src, dst, send, recv, target):
        return pltpu.make_async_remote_copy(
            src_ref=src, dst_ref=dst, send_sem=send, recv_sem=recv,
            device_id=target, device_id_type=MESH)

    def g_rows(piece, part_at):
        return pl.ds(pl.multiple_of(piece * gp_len + part_at * gh, gh), gh)

    def a_rows(piece, part_at):
        return pl.ds(pl.multiple_of(piece * rp + part_at * ah, ah), ah)

    def g_send(o):
        t = lax.rem(s + o, S)
        return remote(grads.at[t, pl.ds(pl.multiple_of(c * gh, gh), gh)], g_buf.at[g_rows(s, c)],
                      gz_send.at[o], gz_recv.at[s], place(t, c, k))

    def a_send(o):
        t = lax.rem(s + o, S)
        return remote(act.at[t, pl.ds(pl.multiple_of(k * ah, ah), ah)], a_buf.at[a_rows(s, k)],
                      az_send.at[o], az_recv.at[s], place(t, c, k))

    def g_pass(piece, m):
        return remote(g_buf.at[g_rows(piece, c)], g_buf.at[g_rows(piece, c)],
                      gx_send.at[piece, m], gx_recv.at[piece, c], place(s, lax.rem(c + m, C), k))

    def a_pass(piece, m):
        rows = a_rows(piece, k)
        return remote(a_buf.at[rows], a_buf.at[rows], ax_send.at[piece, m],
                      ax_recv.at[piece, k], place(s, c, lax.rem(k + m, E)))

    def arrived(ref, sem):
        pltpu.make_async_copy(ref, ref, sem).wait()

    def pieces(step):
        each(S, lambda o: step(o, lax.rem(s - o + S, S)))

    each(S, lambda o: g_send(o).start())
    for copy in local[3:]:
        copy.start()

    for copy in local[:2]:
        copy.wait()
    per_q = kept // Q
    ring[pl.ds(me, 1)] = jnp.zeros((1, 8, kept), I32)
    for q in range(Q):
        ring[me, 0:1, q * per_q:(q + 1) * per_q] = begins[...]
        ring[me, 1:2, q * per_q:(q + 1) * per_q] = halves[...]

    def r_copy(m):
        return remote(ring.at[me], ring.at[me], r_send.at[m], r_recv.at[me],
                      spot(s, lax.rem(me + m, Q)))

    each(Q, lambda m: r_copy(m).start())

    local[2].wait()
    width = out_width // kept
    kept_cols = columns[...] + iota((1, kept), 1) * width

    def tabulate(b, carry):
        at = iota((word_count, kept), 0) * BITS + b
        full = ((jnp.right_shift(at, log2(gp_len)) * E + k) * gp_len
                + jnp.bitwise_and(at, gp_len - 1))
        table[pl.ds(pl.multiple_of(b * word_count, word_count), word_count), :] = sign_of(
            jnp.bitwise_and(full, kept_cols)).astype(BF16)
        return carry

    lax.fori_loop(0, BITS, tabulate, 0)
    hada[...] = sign_of(jnp.bitwise_and(
        iota((row_block, row_block), 0), iota((row_block, row_block), 1))).astype(BF16)

    block = perm.shape[0]
    block_words = block // BITS
    blocks = total_cols // block
    row_at, col_at = iota((block, block), 0), iota((block, block), 1)
    source = (jnp.bitwise_and(row_at, block_words - 1) * BITS
              + jnp.right_shift(row_at, log2(block_words)))
    perm[...] = jnp.where(col_at == source, 1.0, 0.0).astype(BF16)

    def permute(at):
        rows = g_buf[pl.ds(pl.multiple_of(at * block, block), block), :]
        moved = jnp.dot(perm[...], rows, preferred_element_type=F32).astype(BF16)
        for b in range(BITS):
            gp[pl.ds(pl.multiple_of(b * word_count + at * block_words, block_words),
                     block_words), :] = moved[b * block_words:(b + 1) * block_words]

    def g_step(o, piece):
        arrived(g_buf.at[g_rows(piece, c)], gz_recv.at[piece])
        a_send(o).start()
        each(C, lambda m: g_pass(piece, m).start())

    pieces(g_step)
    local[3].wait()
    piece_blocks = block == gp_len

    def g_whole(o, carry):
        piece = lax.rem(s - o + S, S)

        @pl.when(o > 0)
        def _():
            def wait(m):
                other = lax.rem(c + m, C)
                arrived(g_buf.at[g_rows(piece, other)], gx_recv.at[piece, other])
            each(C, wait)
        if piece_blocks:
            permute(piece)
        return carry

    lax.fori_loop(0, S, g_whole, 0)
    if not piece_blocks:
        lax.fori_loop(0, blocks, lambda at, _: (permute(at), 0)[1], 0)
    wide = min(WIDE, total_cols)

    def turn(at, carry):
        here = pl.ds(pl.multiple_of(at * wide, wide), wide)
        gt[:, here] = gp[here, :].T
        return carry

    lax.fori_loop(0, total_cols // wide, turn, 0)

    def score_rows(row):
        here = pl.ds(pl.multiple_of(row, row_block), row_block)
        a = a_buf[here, :]
        w = words[here, :]
        total = jnp.zeros((row_block, kept), F32)
        for at in range(total_cols // wide):
            grad = jnp.dot(a, gt[:, at * wide:(at + 1) * wide], preferred_element_type=F32)
            signed = []
            for bb in range(wide // word_count):
                bit = 1 << (at * (wide // word_count) + bb)
                one = grad[:, bb * word_count:(bb + 1) * word_count]
                signed.append(jnp.where(jnp.bitwise_and(w, bit) != 0, -one, one))
            high, low = split(jnp.concatenate(signed, axis=1))
            side = table[at * wide:(at + 1) * wide, :]
            total = total + jnp.dot(high, side, preferred_element_type=F32)
            total = total + jnp.dot(low, side, preferred_element_type=F32)
        got = jnp.dot(hada[...], jnp.concatenate(split(total), axis=1),
                      preferred_element_type=F32)
        part[here, :] = got[:, :kept] + got[:, kept:]

    local[4].wait()
    local[5].wait()

    def a_step(n, carry):
        o, m = lax.div(n, E), lax.rem(n, E)
        piece = lax.rem(s - o + S, S)
        other = lax.rem(k + m, E)

        @pl.when(jnp.logical_and(o > 0, m == 0))
        def _():
            arrived(a_buf.at[a_rows(piece, k)], az_recv.at[piece])
            each(E, lambda at: a_pass(piece, at).start())

        @pl.when(jnp.logical_and(o > 0, m > 0))
        def _():
            arrived(a_buf.at[a_rows(piece, other)], ax_recv.at[piece, other])

        def rows(at, inner):
            score_rows(piece * rp + other * ah + at * row_block)
            return inner

        lax.fori_loop(0, ah // row_block, rows, 0)
        return carry

    lax.fori_loop(0, S * E, a_step, 0)

    mixed = [part[at:at + row_block, :] for at in range(0, total_rows, row_block)]
    step = 1
    while step < len(mixed):
        nxt = list(mixed)
        for at in range(len(mixed)):
            if at & step == 0:
                nxt[at] = mixed[at] + mixed[at + step]
                nxt[at + step] = mixed[at] - mixed[at + step]
        mixed = nxt
        step *= 2
    whole = mixed if row_block >= LANES else [
        jnp.concatenate(mixed[at:at + LANES // row_block], axis=0)
        for at in range(0, len(mixed), LANES // row_block)]
    turned_rows = 0
    for values in whole:
        for b in range(0, values.shape[0], LANES):
            turned[turned_rows:turned_rows + LANES, :] = values[b:b + LANES, :].T
            turned_rows += LANES

    def r_arrived(m):
        q = lax.rem(me + m, Q)
        arrived(ring.at[q], r_recv.at[q])

    each(Q, r_arrived)
    lane = iota((1, kept), 1)
    begin = jnp.zeros((1, kept), I32)
    half = jnp.zeros((1, kept), I32)
    for q in range(Q):
        mine = jnp.right_shift(lane, log2(per_q)) == q
        begin = jnp.where(mine, ring[q, 0:1, :], begin)
        half = jnp.where(mine, ring[q, 1:2, :], half)
    fold = LANES // kr
    high_rows = kept // fold
    shape = (high_rows, LANES)
    wide_lane = iota(shape, 1)
    at_i = jnp.bitwise_and(wide_lane, kr - 1)
    group = jnp.right_shift(wide_lane, log2(kr))

    def down(vector):
        plain[...] = jnp.broadcast_to(vector, (kept, kept)).T
        got = plain[pl.ds(0, high_rows, stride=fold), :]
        for f in range(1, fold):
            got = jnp.where(group == f, plain[pl.ds(f, high_rows, stride=fold), :], got)
        return got

    row = jnp.bitwise_and(down(begin) + at_i * (2 * down(half) + 1), in_width - 1)
    piece_bits, context_bits = log2(rp), log2(C)
    sign = sign_of(jnp.bitwise_and(jnp.bitwise_and(jnp.right_shift(row, piece_bits), C - 1), c))
    held = (jnp.left_shift(jnp.right_shift(row, piece_bits + context_bits), piece_bits)
            + jnp.bitwise_and(row, rp - 1))
    in_block = jnp.bitwise_and(held, LANES - 1)
    which = jnp.right_shift(held, log2(LANES))
    picked = jnp.zeros(shape, F32)
    for at in range(total_rows // LANES):
        found = None
        for f in range(fold):
            values = turned[pl.ds(at * LANES + f, high_rows, stride=fold), :]
            got = jnp.take_along_axis(values, in_block, axis=1, mode="promise_in_bounds")
            found = got if found is None else jnp.where(group == f, got, found)
        picked = jnp.where(which == at, found, picked)
    sketch[...] = picked * sign * scale

    per = high_rows // Q
    mine_at = s * Q + me

    def q_rows(q):
        return pl.ds(pl.multiple_of(q * per, per), per)

    def p_copy(m):
        t, q = member(jnp.int32(m))
        return remote(sketch.at[q_rows(q)], parts.at[mine_at], p_send.at[m], p_recv.at[mine_at],
                      spot(t, q))

    each(S * Q, lambda m: p_copy(m).start())
    parts[pl.ds(mine_at, 1)] = sketch[q_rows(me), :][None]
    local[6].wait()

    def p_arrived(m):
        t, q = member(jnp.int32(m))
        arrived(parts.at[t * Q + q], p_recv.at[t * Q + q])

    each(S * Q, p_arrived)
    nvl = val.shape[0]
    nv = nvl * S
    out_lane = iota((1, LANES), 1)

    def products(e):
        own = parts[e * Q]
        for q in range(1, Q):
            own = own + parts[e * Q + q]
        total = jnp.zeros((nvl, LANES), F32)
        for r in range(per):
            total = total + val[:, r * LANES:(r + 1) * LANES] * own[r:r + 1, :]
        squares = jnp.sum(own * own, axis=0, keepdims=True)
        tall = jnp.concatenate(
            [total, squares, jnp.zeros((LANES - nvl - 1, LANES), F32)], axis=0)
        line = jnp.sum(tall.T, axis=0, keepdims=True)
        norm = jnp.sum(squares, axis=1, keepdims=True)
        mine = pltpu.roll(jnp.where(out_lane < nvl, line, 0.0), s * nvl, axis=1)
        mine = jnp.where(out_lane == nv, norm * (s == 0).astype(F32), mine)
        return jnp.broadcast_to(mine, (8, LANES))

    answers = part

    def e_rows(e):
        return pl.ds(pl.multiple_of(e * 8, 8), 8)

    def put(e, carry):
        answers[e_rows(e), :] = products(e)
        return carry

    lax.fori_loop(0, S, put, 0)

    def s_copy(m):
        t, q = member(jnp.int32(m))
        return remote(answers.at[e_rows(t)], sums.at[mine_at], s_send.at[m], s_recv.at[mine_at],
                      spot(t, q))

    each(S * Q, lambda m: s_copy(m).start())
    sums[pl.ds(mine_at, 1)] = answers[e_rows(s), :][None]

    def s_arrived(m):
        t, q = member(jnp.int32(m))
        arrived(sums.at[t * Q + q], s_recv.at[t * Q + q])

    each(S * Q, s_arrived)
    all_sums = sums[0]
    for at in range(1, S * Q):
        all_sums = all_sums + sums[at]
    out[...] = all_sums[0:1, :nv] / jnp.sqrt(all_sums[0:1, nv:nv + 1] + 1e-06)

    def sent(o, piece):
        g_send(o).wait_send()
        a_send(o).wait_send()
        each(C, lambda m: g_pass(piece, m).wait_send())
        each(E, lambda m: a_pass(piece, m).wait_send())

    pieces(sent)
    each(Q, lambda m: r_copy(m).wait_send())
    each(S * Q, lambda m: p_copy(m).wait_send())
    each(S * Q, lambda m: s_copy(m).wait_send())


def body(activations, out_grads, sign_bits, keep_cols, row_start, row_step, val_sketch):
    S, C, E = lax.axis_size("sketch"), lax.axis_size("context"), lax.axis_size("example")
    Q = C * E
    rp, tokens = activations.shape[1:]
    gp_len = out_grads.shape[1]
    local_rows, local_cols = S * rp, S * gp_len
    in_width, out_width = local_rows * C, local_cols * E
    kept = keep_cols.shape[0]
    keep = val_sketch.shape[1] * Q
    kr = keep // kept
    nv = val_sketch.shape[0] * S
    words = sign_bits.reshape(local_rows, -1)
    row_block = min(ROWS, rp // E)
    hbm = pl.BlockSpec(memory_space=pl.ANY)
    dma = pltpu.SemaphoreType.DMA
    block = min(WIDE, local_cols)
    return pl.pallas_call(
        functools.partial(
            kernel, (S, C, E), 1.0 / (math.sqrt(in_width) * math.sqrt(out_width)), kr),
        out_shape=jax.ShapeDtypeStruct((1, nv), F32),
        in_specs=[hbm] * 7,
        out_specs=pl.BlockSpec(memory_space=pltpu.VMEM),
        scratch_shapes=[
            pltpu.VMEM((local_rows, tokens), BF16),
            pltpu.VMEM((local_cols, tokens), BF16),
            pltpu.VMEM((local_cols, tokens), BF16),
            pltpu.VMEM((tokens, local_cols), BF16),
            pltpu.VMEM((local_cols, kept), BF16),
            pltpu.VMEM((block, block), BF16),
            pltpu.VMEM((row_block, row_block), BF16),
            pltpu.VMEM(words.shape, I32),
            pltpu.VMEM((1, kept), I32),
            pltpu.VMEM((1, kept // Q), I32),
            pltpu.VMEM((1, kept // Q), I32),
            pltpu.VMEM(val_sketch.shape, F32),
            pltpu.VMEM((local_rows, kept), F32),
            pltpu.VMEM((local_rows, LANES), F32),
            pltpu.VMEM((kept, kept), I32),
            pltpu.VMEM((Q, 8, kept), I32),
            pltpu.VMEM((keep // LANES, LANES), F32),
            pltpu.VMEM((S * Q, keep // LANES // Q, LANES), F32),
            pltpu.VMEM((S * Q, 8, LANES), F32),
            dma((7,)),
            dma((S,)), dma((S,)), dma((S,)), dma((S,)),
            dma((S, C)), dma((S, C)), dma((S, E)), dma((S, E)),
            dma((Q,)), dma((Q,)),
            dma((S * Q,)), dma((S * Q,)), dma((S * Q,)), dma((S * Q,)),
        ],
        compiler_params=pltpu.CompilerParams(
            collective_id=0, has_side_effects=True, vmem_limit_bytes=60 * 2**20),
        cost_estimate=pl.CostEstimate(
            flops=2 * local_rows * local_cols * (tokens + 2 * kept),
            bytes_accessed=2 * (local_rows + local_cols) * tokens, transcendentals=0),
        name="scores",
    )(activations, out_grads, words, keep_cols[None], row_start[None], row_step[None], val_sketch)


def solution(mesh):
    placed = (
        P("groups", ("sketch", "context"), None),
        P("groups", ("sketch", "example"), None),
        P(None, "context", None, "example", None),
        P(),
        P(("context", "example")),
        P(("context", "example")),
        P("sketch", ("context", "example")),
    )
    return jax.shard_map(
        body, mesh=mesh, in_specs=placed, out_specs=P(("groups", "sketch"), None), check_vma=False
    )
```

```python
import functools
import math

import jax
import jax.numpy as jnp
from jax import lax
from jax.experimental import pallas as pl
from jax.experimental.pallas import tpu as pltpu
from jax.sharding import PartitionSpec as P

MESH = pl.DeviceIdType.MESH
F32 = jnp.float32
BF16 = jnp.bfloat16
I32 = jnp.int32
LANES = 128
BITS = 16
ROWS = 256
WIDE = 512
WINDOW = 3


def log2(n):
    return n.bit_length() - 1


def sign_of(common):
    for shift in (16, 8, 4, 2, 1):
        common = jnp.bitwise_xor(common, jnp.right_shift(common, shift))
    return (1 - 2 * jnp.bitwise_and(common, 1)).astype(F32)


def iota(shape, axis):
    return lax.broadcasted_iota(I32, shape, axis)


def split(values):
    high = values.astype(BF16)
    return high, (values - high.astype(F32)).astype(BF16)


def place(s, c, k):
    return {"sketch": s, "context": c, "example": k}


def each(count, step):
    if count <= 16:
        for at in range(1, count):
            step(at)
    else:
        lax.fori_loop(1, count, lambda at, _: (step(at), 0)[1], 0)


def wrap(at, size):
    return jnp.bitwise_and(at, size - 1)


def kernel(sizes, scale, kr, act, grads, words_in, columns_in, begin_in, half_in, val_in, out,
           a_buf, g_buf, gp, gt, table, perm, hada, words, columns, begins, halves, val,
           part, turned, plain, ring, sketch, parts, sums,
           own_sem, gz_send, gz_recv, az_send, az_recv, gx_send, gx_recv, ax_send, ax_recv,
           r_send, r_recv, p_send, p_recv, s_send, s_recv):
    S, C, E = sizes
    Q = C * E
    s, c, k = lax.axis_index("sketch"), lax.axis_index("context"), lax.axis_index("example")
    me = c * E + k
    rp, gp_len = act.shape[1], grads.shape[1]
    gh = gp_len // C
    row_block = min(ROWS, rp)
    parts_of = rp // row_block
    ah = row_block // E
    total_rows, total_cols = a_buf.shape[0], g_buf.shape[0]
    in_width, out_width = total_rows * C, total_cols * E
    word_count = words.shape[1]
    kept = columns.shape[1]

    def member(m):
        m = jnp.int32(m)
        return wrap(s + jnp.right_shift(m, log2(Q)), S), wrap(me + m, Q)

    def spot(t, q):
        return place(t, jnp.right_shift(q, log2(E)), wrap(q, E))

    barrier = pltpu.get_barrier_semaphore()

    def greet(m):
        pl.semaphore_signal(barrier, inc=1, device_id=spot(*member(m)),
                            device_id_type=MESH)

    local = [
        pltpu.make_async_copy(src, dst, own_sem.at[at]) for at, (src, dst) in enumerate((
            (begin_in, begins), (half_in, halves), (columns_in, columns),
            (grads.at[s], g_buf.at[pl.ds(pl.multiple_of(s * gp_len, gp_len), gp_len)]),
            (act.at[s], a_buf.at[pl.ds(pl.multiple_of(s * rp, rp), rp)]),
            (words_in, words), (val_in, val)))
    ]
    each(S * Q, greet)
    for copy in local:
        copy.start()
    pl.semaphore_wait(barrier, S * Q - 1)

    def remote(src, dst, send, recv, target):
        return pltpu.make_async_remote_copy(
            src_ref=src, dst_ref=dst, send_sem=send, recv_sem=recv,
            device_id=target, device_id_type=MESH)

    def g_rows(piece, part_at):
        return pl.ds(pl.multiple_of(piece * gp_len + part_at * gh, gh), gh)

    def a_rows(piece, h, part_at):
        return pl.ds(pl.multiple_of(piece * rp + h * row_block + part_at * ah, ah), ah)

    def nth(n):
        n = jnp.int32(n)
        return 1 + jnp.right_shift(n, log2(parts_of)), wrap(n, parts_of)

    def g_send(o):
        t = wrap(s + o, S)
        return remote(grads.at[t, pl.ds(pl.multiple_of(c * gh, gh), gh)], g_buf.at[g_rows(s, c)],
                      gz_send.at[o], gz_recv.at[s], place(t, c, k))

    def a_send(n):
        o, h = nth(n)
        t = wrap(s + o, S)
        return remote(act.at[t, pl.ds(pl.multiple_of(h * row_block + k * ah, ah), ah)],
                      a_buf.at[a_rows(s, h, k)], az_send.at[n], az_recv.at[s, h],
                      place(t, c, k))

    def g_pass(piece, m):
        return remote(g_buf.at[g_rows(piece, c)], g_buf.at[g_rows(piece, c)],
                      gx_send.at[piece, m], gx_recv.at[piece, c], place(s, wrap(c + m, C), k))

    def a_pass(piece, h, m):
        rows = a_rows(piece, h, k)
        return remote(a_buf.at[rows], a_buf.at[rows], ax_send.at[piece, h, m],
                      ax_recv.at[piece, h, k], place(s, c, wrap(k + m, E)))

    def arrived(ref, sem):
        pltpu.make_async_copy(ref, ref, sem).wait()

    def pieces(step):
        each(S, lambda o: step(o, wrap(s - o + S, S)))

    each(S, lambda o: g_send(o).start())
    a_send(0).start()

    for copy in local[:2]:
        copy.wait()
    per_q = kept // Q
    ring[pl.ds(me, 1)] = jnp.zeros((1, 8, kept), I32)
    for q in range(Q):
        ring[me, 0:1, q * per_q:(q + 1) * per_q] = begins[...]
        ring[me, 1:2, q * per_q:(q + 1) * per_q] = halves[...]

    def r_copy(m):
        return remote(ring.at[me], ring.at[me], r_send.at[m], r_recv.at[me],
                      spot(s, wrap(me + m, Q)))

    each(Q, lambda m: r_copy(m).start())

    local[2].wait()
    width = out_width // kept
    kept_cols = columns[...] + iota((1, kept), 1) * width

    def tabulate(b, carry):
        at = iota((word_count, kept), 0) * BITS + b
        full = ((jnp.right_shift(at, log2(gp_len)) * E + k) * gp_len
                + jnp.bitwise_and(at, gp_len - 1))
        table[pl.ds(pl.multiple_of(b * word_count, word_count), word_count), :] = sign_of(
            jnp.bitwise_and(full, kept_cols)).astype(BF16)
        return carry

    lax.fori_loop(0, BITS, tabulate, 0)
    hada[...] = sign_of(jnp.bitwise_and(
        iota((row_block, row_block), 0), iota((row_block, row_block), 1))).astype(BF16)

    block = perm.shape[0]
    block_words = block // BITS
    blocks = total_cols // block
    row_at, col_at = iota((block, block), 0), iota((block, block), 1)
    source = (jnp.bitwise_and(row_at, block_words - 1) * BITS
              + jnp.right_shift(row_at, log2(block_words)))
    perm[...] = jnp.where(col_at == source, 1.0, 0.0).astype(BF16)

    def permute(at):
        rows = g_buf[pl.ds(pl.multiple_of(at * block, block), block), :]
        moved = jnp.dot(perm[...], rows, preferred_element_type=F32).astype(BF16)
        for b in range(BITS):
            gp[pl.ds(pl.multiple_of(b * word_count + at * block_words, block_words),
                     block_words), :] = moved[b * block_words:(b + 1) * block_words]

    def g_step(o, piece):
        arrived(g_buf.at[g_rows(piece, c)], gz_recv.at[piece])
        each(C, lambda m: g_pass(piece, m).start())
        if isinstance(o, int) and o < min(WINDOW, a_count):
            a_send(o).start()

    a_count = (S - 1) * parts_of
    pieces(g_step)
    if S > 16:
        for n in range(1, min(WINDOW, a_count)):
            a_send(n).start()
    local[3].wait()
    piece_blocks = block == gp_len

    def g_whole(o, carry):
        piece = wrap(s - o + S, S)

        @pl.when(o > 0)
        def _():
            def wait(m):
                other = wrap(c + m, C)
                arrived(g_buf.at[g_rows(piece, other)], gx_recv.at[piece, other])
            each(C, wait)
        if piece_blocks:
            permute(piece)
        return carry

    lax.fori_loop(0, S, g_whole, 0)
    if not piece_blocks:
        lax.fori_loop(0, blocks, lambda at, _: (permute(at), 0)[1], 0)
    wide = min(WIDE, total_cols)

    def turn(at, carry):
        here = pl.ds(pl.multiple_of(at * wide, wide), wide)
        gt[:, here] = gp[here, :].T
        return carry

    lax.fori_loop(0, total_cols // wide, turn, 0)

    def score_rows(row):
        here = pl.ds(pl.multiple_of(row, row_block), row_block)
        a = a_buf[here, :]
        w = words[here, :]
        total = jnp.zeros((row_block, kept), F32)
        for at in range(total_cols // wide):
            grad = jnp.dot(a, gt[:, at * wide:(at + 1) * wide], preferred_element_type=F32)
            signed = []
            for bb in range(wide // word_count):
                bit = 1 << (at * (wide // word_count) + bb)
                one = grad[:, bb * word_count:(bb + 1) * word_count]
                signed.append(jnp.where(jnp.bitwise_and(w, bit) != 0, -one, one))
            high, low = split(jnp.concatenate(signed, axis=1))
            side = table[at * wide:(at + 1) * wide, :]
            total = total + jnp.dot(high, side, preferred_element_type=F32)
            total = total + jnp.dot(low, side, preferred_element_type=F32)
        got = jnp.dot(hada[...], jnp.concatenate(split(total), axis=1),
                      preferred_element_type=F32)
        part[here, :] = got[:, :kept] + got[:, kept:]

    local[4].wait()
    local[5].wait()

    def a_step(n, carry):
        o, h = nth(n - parts_of)
        piece = wrap(s - o + S, S)
        n_next = n - parts_of + 1
        o_next, h_next = nth(n_next)
        next_piece = wrap(s - o_next + S, S)

        @pl.when(jnp.logical_and(n_next >= 0, n_next < a_count))
        def _():
            arrived(a_buf.at[a_rows(next_piece, h_next, k)], az_recv.at[next_piece, h_next])
            each(E, lambda m: a_pass(next_piece, h_next, m).start())

        @pl.when(jnp.logical_and(n_next >= 0, n_next + WINDOW < a_count))
        def _():
            a_send(n_next + WINDOW).start()

        @pl.when(n >= parts_of)
        def _():
            def wait(m):
                other = wrap(k + m, E)
                arrived(a_buf.at[a_rows(piece, h, other)], ax_recv.at[piece, h, other])
            each(E, wait)

        score_rows(piece * rp + h * row_block)
        return carry

    lax.fori_loop(0, S * parts_of, a_step, 0)

    mixed = [part[at:at + row_block, :] for at in range(0, total_rows, row_block)]
    step = 1
    while step < len(mixed):
        nxt = list(mixed)
        for at in range(len(mixed)):
            if at & step == 0:
                nxt[at] = mixed[at] + mixed[at + step]
                nxt[at + step] = mixed[at] - mixed[at + step]
        mixed = nxt
        step *= 2
    whole = mixed if row_block >= LANES else [
        jnp.concatenate(mixed[at:at + LANES // row_block], axis=0)
        for at in range(0, len(mixed), LANES // row_block)]
    turned_rows = 0
    for values in whole:
        for b in range(0, values.shape[0], LANES):
            turned[turned_rows:turned_rows + LANES, :] = values[b:b + LANES, :].T
            turned_rows += LANES

    def r_arrived(m):
        q = wrap(me + m, Q)
        arrived(ring.at[q], r_recv.at[q])

    each(Q, r_arrived)
    lane = iota((1, kept), 1)
    begin = jnp.zeros((1, kept), I32)
    half = jnp.zeros((1, kept), I32)
    for q in range(Q):
        mine = jnp.right_shift(lane, log2(per_q)) == q
        begin = jnp.where(mine, ring[q, 0:1, :], begin)
        half = jnp.where(mine, ring[q, 1:2, :], half)
    fold = LANES // kr
    high_rows = kept // fold
    shape = (high_rows, LANES)
    wide_lane = iota(shape, 1)
    at_i = jnp.bitwise_and(wide_lane, kr - 1)
    group = jnp.right_shift(wide_lane, log2(kr))

    def down(vector):
        plain[...] = jnp.broadcast_to(vector, (kept, kept)).T
        got = plain[pl.ds(0, high_rows, stride=fold), :]
        for f in range(1, fold):
            got = jnp.where(group == f, plain[pl.ds(f, high_rows, stride=fold), :], got)
        return got

    row = jnp.bitwise_and(down(begin) + at_i * (2 * down(half) + 1), in_width - 1)
    piece_bits, context_bits = log2(rp), log2(C)
    sign = sign_of(jnp.bitwise_and(jnp.bitwise_and(jnp.right_shift(row, piece_bits), C - 1), c))
    held = (jnp.left_shift(jnp.right_shift(row, piece_bits + context_bits), piece_bits)
            + jnp.bitwise_and(row, rp - 1))
    in_block = jnp.bitwise_and(held, LANES - 1)
    which = jnp.right_shift(held, log2(LANES))
    picked = jnp.zeros(shape, F32)
    for at in range(total_rows // LANES):
        found = None
        for f in range(fold):
            values = turned[pl.ds(at * LANES + f, high_rows, stride=fold), :]
            got = jnp.take_along_axis(values, in_block, axis=1, mode="promise_in_bounds")
            found = got if found is None else jnp.where(group == f, got, found)
        picked = jnp.where(which == at, found, picked)
    sketch[...] = picked * sign * scale

    per = high_rows // Q
    mine_at = s * Q + me

    def q_rows(q):
        return pl.ds(pl.multiple_of(q * per, per), per)

    def p_copy(m):
        t, q = member(m)
        return remote(sketch.at[q_rows(q)], parts.at[mine_at], p_send.at[0], p_recv.at[0],
                      spot(t, q))

    each(S * Q, lambda m: p_copy(m).start())
    parts[pl.ds(mine_at, 1)] = sketch[q_rows(me), :][None]
    local[6].wait()

    def sent(o, piece):
        g_send(o).wait_send()
        each(C, lambda m: g_pass(piece, m).wait_send())
        for h in range(parts_of):
            each(E, lambda m: a_pass(piece, h, m).wait_send())

    pieces(sent)
    each(a_count + 1, lambda n: a_send(n - 1).wait_send())
    each(Q, lambda m: r_copy(m).wait_send())
    others = pl.ds(0, S * Q - 1)
    arrived(parts.at[others], p_recv.at[0])
    nvl = val.shape[0]
    nv = nvl * S
    out_lane = iota((1, LANES), 1)

    def products(e):
        own = parts[e * Q]
        for q in range(1, Q):
            own = own + parts[e * Q + q]
        total = jnp.zeros((nvl, LANES), F32)
        for r in range(per):
            total = total + val[:, r * LANES:(r + 1) * LANES] * own[r:r + 1, :]
        squares = jnp.sum(own * own, axis=0, keepdims=True)
        tall = jnp.concatenate(
            [total, squares, jnp.zeros((LANES - nvl - 1, LANES), F32)], axis=0)
        line = jnp.sum(tall.T, axis=0, keepdims=True)
        norm = jnp.sum(squares, axis=1, keepdims=True)
        mine = pltpu.roll(jnp.where(out_lane < nvl, line, 0.0), s * nvl, axis=1)
        mine = jnp.where(out_lane == nv, norm * (s == 0).astype(F32), mine)
        return jnp.broadcast_to(mine, (8, LANES))

    answers = part

    def e_rows(e):
        return pl.ds(pl.multiple_of(e * 8, 8), 8)

    def put(e, carry):
        answers[e_rows(e), :] = products(e)
        return carry

    lax.fori_loop(0, S, put, 0)

    def s_copy(m):
        t, q = member(m)
        return remote(answers.at[e_rows(t)], sums.at[mine_at], s_send.at[0], s_recv.at[0],
                      spot(t, q))

    each(S * Q, lambda m: s_copy(m).start())
    sums[pl.ds(mine_at, 1)] = answers[e_rows(s), :][None]

    arrived(sums.at[others], s_recv.at[0])
    all_sums = sums[0]
    for at in range(1, S * Q):
        all_sums = all_sums + sums[at]
    out[...] = all_sums[0:1, :nv] / jnp.sqrt(all_sums[0:1, nv:nv + 1] + 1e-06)
    arrived(parts.at[others], p_send.at[0])
    arrived(sums.at[others], s_send.at[0])


def body(activations, out_grads, sign_bits, keep_cols, row_start, row_step, val_sketch):
    S, C, E = lax.axis_size("sketch"), lax.axis_size("context"), lax.axis_size("example")
    Q = C * E
    rp, tokens = activations.shape[1:]
    gp_len = out_grads.shape[1]
    local_rows, local_cols = S * rp, S * gp_len
    in_width, out_width = local_rows * C, local_cols * E
    kept = keep_cols.shape[0]
    keep = val_sketch.shape[1] * Q
    kr = keep // kept
    nv = val_sketch.shape[0] * S
    words = sign_bits.reshape(local_rows, -1)
    row_block = min(ROWS, rp)
    parts_of = rp // row_block
    a_count = (S - 1) * parts_of
    hbm = pl.BlockSpec(memory_space=pl.ANY)
    dma = pltpu.SemaphoreType.DMA
    block = min(WIDE, local_cols)
    return pl.pallas_call(
        functools.partial(
            kernel, (S, C, E), 1.0 / (math.sqrt(in_width) * math.sqrt(out_width)), kr),
        out_shape=jax.ShapeDtypeStruct((1, nv), F32),
        in_specs=[hbm] * 7,
        out_specs=pl.BlockSpec(memory_space=pltpu.VMEM),
        scratch_shapes=[
            pltpu.VMEM((local_rows, tokens), BF16),
            pltpu.VMEM((local_cols, tokens), BF16),
            pltpu.VMEM((local_cols, tokens), BF16),
            pltpu.VMEM((tokens, local_cols), BF16),
            pltpu.VMEM((local_cols, kept), BF16),
            pltpu.VMEM((block, block), BF16),
            pltpu.VMEM((row_block, row_block), BF16),
            pltpu.VMEM(words.shape, I32),
            pltpu.VMEM((1, kept), I32),
            pltpu.VMEM((1, kept // Q), I32),
            pltpu.VMEM((1, kept // Q), I32),
            pltpu.VMEM(val_sketch.shape, F32),
            pltpu.VMEM((local_rows, kept), F32),
            pltpu.VMEM((local_rows, LANES), F32),
            pltpu.VMEM((kept, kept), I32),
            pltpu.VMEM((Q, 8, kept), I32),
            pltpu.VMEM((keep // LANES, LANES), F32),
            pltpu.VMEM((S * Q, keep // LANES // Q, LANES), F32),
            pltpu.VMEM((S * Q, 8, LANES), F32),
            dma((7,)),
            dma((S,)), dma((S,)), dma((a_count,)), dma((S, parts_of)),
            dma((S, C)), dma((S, C)), dma((S, parts_of, E)), dma((S, parts_of, E)),
            dma((Q,)), dma((Q,)),
            dma((1,)), dma((1,)), dma((1,)), dma((1,)),
        ],
        compiler_params=pltpu.CompilerParams(
            collective_id=0, has_side_effects=True, vmem_limit_bytes=60 * 2**20),
        cost_estimate=pl.CostEstimate(
            flops=2 * local_rows * local_cols * (tokens + 2 * kept),
            bytes_accessed=2 * (local_rows + local_cols) * tokens, transcendentals=0),
        name="scores",
    )(activations, out_grads, words, keep_cols[None], row_start[None], row_step[None], val_sketch)


def solution(mesh):
    placed = (
        P("groups", ("sketch", "context"), None),
        P("groups", ("sketch", "example"), None),
        P(None, "context", None, "example", None),
        P(),
        P(("context", "example")),
        P(("context", "example")),
        P("sketch", ("context", "example")),
    )
    return jax.shard_map(
        body, mesh=mesh, in_specs=placed, out_specs=P(("groups", "sketch"), None), check_vma=False
    )
```

```python
import functools
import math

import jax
import jax.numpy as jnp
from jax import lax
from jax.experimental import pallas as pl
from jax.experimental.pallas import tpu as pltpu
from jax.sharding import PartitionSpec as P

MESH = pl.DeviceIdType.MESH
F32 = jnp.float32
BF16 = jnp.bfloat16
I32 = jnp.int32
LANES = 128
BITS = 16
ROWS = 256
WIDE = 512
WINDOW = 4


def log2(n):
    return n.bit_length() - 1


def sign_of(common):
    for shift in (16, 8, 4, 2, 1):
        common = jnp.bitwise_xor(common, jnp.right_shift(common, shift))
    return (1 - 2 * jnp.bitwise_and(common, 1)).astype(F32)


def iota(shape, axis):
    return lax.broadcasted_iota(I32, shape, axis)


def split(values):
    high = values.astype(BF16)
    return high, (values - high.astype(F32)).astype(BF16)


def place(s, c, k):
    return {"sketch": s, "context": c, "example": k}


def each(count, step):
    if count <= 16:
        for at in range(1, count):
            step(at)
    else:
        lax.fori_loop(1, count, lambda at, _: (step(at), 0)[1], 0)


def wrap(at, size):
    return jnp.bitwise_and(at, size - 1)


def kernel(sizes, scale, kr, act, grads, words_in, columns_in, begin_in, half_in, val_in, out,
           a_buf, g_buf, gp, gt, table, perm, hada, words, columns, begins, halves, val,
           part, turned, plain, ring, sketch, parts, sums,
           own_sem, gz_send, gz_recv, az_send, az_recv, gx_send, gx_recv, ax_send, ax_recv,
           r_send, r_recv, p_send, p_recv, s_send, s_recv):
    S, C, E = sizes
    Q = C * E
    s, c, k = lax.axis_index("sketch"), lax.axis_index("context"), lax.axis_index("example")
    me = c * E + k
    rp, gp_len = act.shape[1], grads.shape[1]
    gh = gp_len // C
    g_parts = 2 if gh % 64 == 0 else 1
    gq = gh // g_parts
    row_block = min(ROWS, rp)
    parts_of = rp // row_block
    ah = row_block // E
    total_rows, total_cols = a_buf.shape[0], g_buf.shape[0]
    in_width, out_width = total_rows * C, total_cols * E
    word_count = words.shape[1]
    kept = columns.shape[1]

    def member(m):
        m = jnp.int32(m)
        return wrap(s + jnp.right_shift(m, log2(Q)), S), wrap(me + m, Q)

    def spot(t, q):
        return place(t, jnp.right_shift(q, log2(E)), wrap(q, E))

    barrier = pltpu.get_barrier_semaphore()

    def greet(m):
        pl.semaphore_signal(barrier, inc=1, device_id=spot(*member(m)),
                            device_id_type=MESH)

    local = [
        pltpu.make_async_copy(src, dst, own_sem.at[at]) for at, (src, dst) in enumerate((
            (begin_in, begins), (half_in, halves), (columns_in, columns),
            (grads.at[s], g_buf.at[pl.ds(pl.multiple_of(s * gp_len, gp_len), gp_len)]),
            (act.at[s], a_buf.at[pl.ds(pl.multiple_of(s * rp, rp), rp)]),
            (words_in, words), (val_in, val)))
    ]
    each(S * Q, greet)
    for copy in local:
        copy.start()
    pl.semaphore_wait(barrier, S * Q - 1)

    def remote(src, dst, send, recv, target):
        return pltpu.make_async_remote_copy(
            src_ref=src, dst_ref=dst, send_sem=send, recv_sem=recv,
            device_id=target, device_id_type=MESH)

    g_count, a_count = (S - 1) * g_parts, (S - 1) * parts_of

    def g_rows(piece, h, part_at):
        return pl.ds(pl.multiple_of(piece * gp_len + part_at * gh + h * gq, gq), gq)

    def a_rows(piece, h, part_at):
        return pl.ds(pl.multiple_of(piece * rp + h * row_block + part_at * ah, ah), ah)

    def nth(n, parts_in):
        n = jnp.int32(n)
        return 1 + jnp.right_shift(n, log2(parts_in)), wrap(n, parts_in)

    def g_send(n):
        o, h = nth(n, g_parts)
        t = wrap(s + o, S)
        return remote(grads.at[t, pl.ds(pl.multiple_of(c * gh + h * gq, gq), gq)],
                      g_buf.at[g_rows(s, h, c)], gz_send.at[n], gz_recv.at[s, h],
                      place(t, c, k))

    def a_send(n):
        o, h = nth(n, parts_of)
        t = wrap(s + o, S)
        return remote(act.at[t, pl.ds(pl.multiple_of(h * row_block + k * ah, ah), ah)],
                      a_buf.at[a_rows(s, h, k)], az_send.at[n], az_recv.at[s, h],
                      place(t, c, k))

    def g_pass(piece, h, m):
        rows = g_rows(piece, h, c)
        return remote(g_buf.at[rows], g_buf.at[rows], gx_send.at[piece, h, m],
                      gx_recv.at[piece, h, c], place(s, wrap(c + m, C), k))

    def a_pass(piece, h, m):
        rows = a_rows(piece, h, k)
        return remote(a_buf.at[rows], a_buf.at[rows], ax_send.at[piece, h, m],
                      ax_recv.at[piece, h, k], place(s, c, wrap(k + m, E)))

    def arrived(ref, sem):
        pltpu.make_async_copy(ref, ref, sem).wait()

    def pieces(step):
        each(S, lambda o: step(o, wrap(s - o + S, S)))

    def issue(n):
        n = jnp.int32(n)

        @pl.when(n < g_count)
        def _():
            g_send(n).start()

        @pl.when(jnp.logical_and(n >= g_count, n < g_count + a_count))
        def _():
            a_send(n - g_count).start()

    lax.fori_loop(0, WINDOW, lambda n, _: (issue(n), 0)[1], 0)

    for copy in local[:2]:
        copy.wait()
    per_q = kept // Q
    ring[pl.ds(me, 1)] = jnp.zeros((1, 8, kept), I32)
    for q in range(Q):
        ring[me, 0:1, q * per_q:(q + 1) * per_q] = begins[...]
        ring[me, 1:2, q * per_q:(q + 1) * per_q] = halves[...]

    def r_copy(m):
        return remote(ring.at[me], ring.at[me], r_send.at[m], r_recv.at[me],
                      spot(s, wrap(me + m, Q)))

    each(Q, lambda m: r_copy(m).start())

    local[2].wait()
    width = out_width // kept
    kept_cols = columns[...] + iota((1, kept), 1) * width

    def tabulate(b, carry):
        at = iota((word_count, kept), 0) * BITS + b
        full = ((jnp.right_shift(at, log2(gp_len)) * E + k) * gp_len
                + jnp.bitwise_and(at, gp_len - 1))
        table[pl.ds(pl.multiple_of(b * word_count, word_count), word_count), :] = sign_of(
            jnp.bitwise_and(full, kept_cols)).astype(BF16)
        return carry

    lax.fori_loop(0, BITS, tabulate, 0)
    hada[...] = sign_of(jnp.bitwise_and(
        iota((row_block, row_block), 0), iota((row_block, row_block), 1))).astype(BF16)

    block = perm.shape[0]
    block_words = block // BITS
    blocks = total_cols // block
    row_at, col_at = iota((block, block), 0), iota((block, block), 1)
    source = (jnp.bitwise_and(row_at, block_words - 1) * BITS
              + jnp.right_shift(row_at, log2(block_words)))
    perm[...] = jnp.where(col_at == source, 1.0, 0.0).astype(BF16)

    def permute(at):
        rows = g_buf[pl.ds(pl.multiple_of(at * block, block), block), :]
        moved = jnp.dot(perm[...], rows, preferred_element_type=F32).astype(BF16)
        for b in range(BITS):
            gp[pl.ds(pl.multiple_of(b * word_count + at * block_words, block_words),
                     block_words), :] = moved[b * block_words:(b + 1) * block_words]

    piece_blocks = block == gp_len

    def g_whole(o):
        piece = wrap(s - o + S, S)
        for h in range(g_parts):
            def wait(m):
                other = wrap(c + m, C)
                arrived(g_buf.at[g_rows(piece, h, other)], gx_recv.at[piece, h, other])
            each(C, wait)
        if piece_blocks:
            permute(piece)

    def g_step(n, carry):
        o, h = nth(n, g_parts)
        piece = wrap(s - o + S, S)
        arrived(g_buf.at[g_rows(piece, h, c)], gz_recv.at[piece, h])
        each(C, lambda m: g_pass(piece, h, m).start())
        issue(n + WINDOW)

        @pl.when(jnp.logical_and(h == 0, o > 1))
        def _():
            g_whole(o - 1)
        return carry

    local[3].wait()
    if piece_blocks:
        permute(s)
    lax.fori_loop(0, g_count, g_step, 0)
    g_whole(jnp.int32(S - 1))
    if not piece_blocks:
        lax.fori_loop(0, blocks, lambda at, _: (permute(at), 0)[1], 0)
    wide = min(WIDE, total_cols)

    def turn(at, carry):
        here = pl.ds(pl.multiple_of(at * wide, wide), wide)
        gt[:, here] = gp[here, :].T
        return carry

    lax.fori_loop(0, total_cols // wide, turn, 0)

    def score_rows(row):
        here = pl.ds(pl.multiple_of(row, row_block), row_block)
        a = a_buf[here, :]
        w = words[here, :]
        total = jnp.zeros((row_block, kept), F32)
        for at in range(total_cols // wide):
            grad = jnp.dot(a, gt[:, at * wide:(at + 1) * wide], preferred_element_type=F32)
            signed = []
            for bb in range(wide // word_count):
                bit = 1 << (at * (wide // word_count) + bb)
                one = grad[:, bb * word_count:(bb + 1) * word_count]
                signed.append(jnp.where(jnp.bitwise_and(w, bit) != 0, -one, one))
            high, low = split(jnp.concatenate(signed, axis=1))
            side = table[at * wide:(at + 1) * wide, :]
            total = total + jnp.dot(high, side, preferred_element_type=F32)
            total = total + jnp.dot(low, side, preferred_element_type=F32)
        got = jnp.dot(hada[...], jnp.concatenate(split(total), axis=1),
                      preferred_element_type=F32)
        part[here, :] = got[:, :kept] + got[:, kept:]

    local[4].wait()
    local[5].wait()

    def a_step(n, carry):
        o, h = nth(n - parts_of, parts_of)
        piece = wrap(s - o + S, S)
        n_next = n - parts_of + 1
        o_next, h_next = nth(n_next, parts_of)
        next_piece = wrap(s - o_next + S, S)

        @pl.when(jnp.logical_and(n_next >= 0, n_next < a_count))
        def _():
            arrived(a_buf.at[a_rows(next_piece, h_next, k)], az_recv.at[next_piece, h_next])
            each(E, lambda m: a_pass(next_piece, h_next, m).start())
            issue(g_count + n_next + WINDOW)

        @pl.when(n >= parts_of)
        def _():
            def wait(m):
                other = wrap(k + m, E)
                arrived(a_buf.at[a_rows(piece, h, other)], ax_recv.at[piece, h, other])
            each(E, wait)

        score_rows(piece * rp + h * row_block)
        return carry

    lax.fori_loop(0, S * parts_of, a_step, 0)

    mixed = [part[at:at + row_block, :] for at in range(0, total_rows, row_block)]
    step = 1
    while step < len(mixed):
        nxt = list(mixed)
        for at in range(len(mixed)):
            if at & step == 0:
                nxt[at] = mixed[at] + mixed[at + step]
                nxt[at + step] = mixed[at] - mixed[at + step]
        mixed = nxt
        step *= 2
    whole = mixed if row_block >= LANES else [
        jnp.concatenate(mixed[at:at + LANES // row_block], axis=0)
        for at in range(0, len(mixed), LANES // row_block)]
    turned_rows = 0
    for values in whole:
        for b in range(0, values.shape[0], LANES):
            turned[turned_rows:turned_rows + LANES, :] = values[b:b + LANES, :].T
            turned_rows += LANES

    def r_arrived(m):
        q = wrap(me + m, Q)
        arrived(ring.at[q], r_recv.at[q])

    each(Q, r_arrived)
    lane = iota((1, kept), 1)
    begin = jnp.zeros((1, kept), I32)
    half = jnp.zeros((1, kept), I32)
    for q in range(Q):
        mine = jnp.right_shift(lane, log2(per_q)) == q
        begin = jnp.where(mine, ring[q, 0:1, :], begin)
        half = jnp.where(mine, ring[q, 1:2, :], half)
    fold = LANES // kr
    high_rows = kept // fold
    shape = (high_rows, LANES)
    wide_lane = iota(shape, 1)
    at_i = jnp.bitwise_and(wide_lane, kr - 1)
    group = jnp.right_shift(wide_lane, log2(kr))

    def down(vector):
        plain[...] = jnp.broadcast_to(vector, (kept, kept)).T
        got = plain[pl.ds(0, high_rows, stride=fold), :]
        for f in range(1, fold):
            got = jnp.where(group == f, plain[pl.ds(f, high_rows, stride=fold), :], got)
        return got

    row = jnp.bitwise_and(down(begin) + at_i * (2 * down(half) + 1), in_width - 1)
    piece_bits, context_bits = log2(rp), log2(C)
    sign = sign_of(jnp.bitwise_and(jnp.bitwise_and(jnp.right_shift(row, piece_bits), C - 1), c))
    held = (jnp.left_shift(jnp.right_shift(row, piece_bits + context_bits), piece_bits)
            + jnp.bitwise_and(row, rp - 1))
    in_block = jnp.bitwise_and(held, LANES - 1)
    which = jnp.right_shift(held, log2(LANES))
    picked = jnp.zeros(shape, F32)
    for at in range(total_rows // LANES):
        found = None
        for f in range(fold):
            values = turned[pl.ds(at * LANES + f, high_rows, stride=fold), :]
            got = jnp.take_along_axis(values, in_block, axis=1, mode="promise_in_bounds")
            found = got if found is None else jnp.where(group == f, got, found)
        picked = jnp.where(which == at, found, picked)
    sketch[...] = picked * sign * scale

    per = high_rows // Q
    mine_at = s * Q + me

    def q_rows(q):
        return pl.ds(pl.multiple_of(q * per, per), per)

    def p_copy(m):
        t, q = member(m)
        return remote(sketch.at[q_rows(q)], parts.at[mine_at], p_send.at[0], p_recv.at[0],
                      spot(t, q))

    each(S * Q, lambda m: p_copy(m).start())
    parts[pl.ds(mine_at, 1)] = sketch[q_rows(me), :][None]
    local[6].wait()

    def sent(o, piece):
        for h in range(g_parts):
            each(C, lambda m: g_pass(piece, h, m).wait_send())
        for h in range(parts_of):
            each(E, lambda m: a_pass(piece, h, m).wait_send())

    pieces(sent)
    each(g_count + 1, lambda n: g_send(n - 1).wait_send())
    each(a_count + 1, lambda n: a_send(n - 1).wait_send())
    each(Q, lambda m: r_copy(m).wait_send())
    others = pl.ds(0, S * Q - 1)
    arrived(parts.at[others], p_recv.at[0])
    nvl = val.shape[0]
    nv = nvl * S
    out_lane = iota((1, LANES), 1)

    def products(e):
        own = parts[e * Q]
        for q in range(1, Q):
            own = own + parts[e * Q + q]
        total = jnp.zeros((nvl, LANES), F32)
        for r in range(per):
            total = total + val[:, r * LANES:(r + 1) * LANES] * own[r:r + 1, :]
        squares = jnp.sum(own * own, axis=0, keepdims=True)
        tall = jnp.concatenate(
            [total, squares, jnp.zeros((LANES - nvl - 1, LANES), F32)], axis=0)
        line = jnp.sum(tall.T, axis=0, keepdims=True)
        norm = jnp.sum(squares, axis=1, keepdims=True)
        mine = pltpu.roll(jnp.where(out_lane < nvl, line, 0.0), s * nvl, axis=1)
        mine = jnp.where(out_lane == nv, norm * (s == 0).astype(F32), mine)
        return jnp.broadcast_to(mine, (8, LANES))

    answers = part

    def e_rows(e):
        return pl.ds(pl.multiple_of(e * 8, 8), 8)

    def put(e, carry):
        answers[e_rows(e), :] = products(e)
        return carry

    lax.fori_loop(0, S, put, 0)

    def s_copy(m):
        t, q = member(m)
        return remote(answers.at[e_rows(t)], sums.at[mine_at], s_send.at[0], s_recv.at[0],
                      spot(t, q))

    each(S * Q, lambda m: s_copy(m).start())
    sums[pl.ds(mine_at, 1)] = answers[e_rows(s), :][None]

    arrived(sums.at[others], s_recv.at[0])
    all_sums = sums[0]
    for at in range(1, S * Q):
        all_sums = all_sums + sums[at]
    out[...] = all_sums[0:1, :nv] / jnp.sqrt(all_sums[0:1, nv:nv + 1] + 1e-06)
    arrived(parts.at[others], p_send.at[0])
    arrived(sums.at[others], s_send.at[0])


def body(activations, out_grads, sign_bits, keep_cols, row_start, row_step, val_sketch):
    S, C, E = lax.axis_size("sketch"), lax.axis_size("context"), lax.axis_size("example")
    Q = C * E
    rp, tokens = activations.shape[1:]
    gp_len = out_grads.shape[1]
    local_rows, local_cols = S * rp, S * gp_len
    in_width, out_width = local_rows * C, local_cols * E
    kept = keep_cols.shape[0]
    keep = val_sketch.shape[1] * Q
    kr = keep // kept
    nv = val_sketch.shape[0] * S
    words = sign_bits.reshape(local_rows, -1)
    row_block = min(ROWS, rp)
    parts_of = rp // row_block
    a_count = (S - 1) * parts_of
    g_parts = 2 if (gp_len // C) % 64 == 0 else 1
    g_count = (S - 1) * g_parts
    hbm = pl.BlockSpec(memory_space=pl.ANY)
    dma = pltpu.SemaphoreType.DMA
    block = min(WIDE, local_cols)
    return pl.pallas_call(
        functools.partial(
            kernel, (S, C, E), 1.0 / (math.sqrt(in_width) * math.sqrt(out_width)), kr),
        out_shape=jax.ShapeDtypeStruct((1, nv), F32),
        in_specs=[hbm] * 7,
        out_specs=pl.BlockSpec(memory_space=pltpu.VMEM),
        scratch_shapes=[
            pltpu.VMEM((local_rows, tokens), BF16),
            pltpu.VMEM((local_cols, tokens), BF16),
            pltpu.VMEM((local_cols, tokens), BF16),
            pltpu.VMEM((tokens, local_cols), BF16),
            pltpu.VMEM((local_cols, kept), BF16),
            pltpu.VMEM((block, block), BF16),
            pltpu.VMEM((row_block, row_block), BF16),
            pltpu.VMEM(words.shape, I32),
            pltpu.VMEM((1, kept), I32),
            pltpu.VMEM((1, kept // Q), I32),
            pltpu.VMEM((1, kept // Q), I32),
            pltpu.VMEM(val_sketch.shape, F32),
            pltpu.VMEM((local_rows, kept), F32),
            pltpu.VMEM((local_rows, LANES), F32),
            pltpu.VMEM((kept, kept), I32),
            pltpu.VMEM((Q, 8, kept), I32),
            pltpu.VMEM((keep // LANES, LANES), F32),
            pltpu.VMEM((S * Q, keep // LANES // Q, LANES), F32),
            pltpu.VMEM((S * Q, 8, LANES), F32),
            dma((7,)),
            dma((g_count,)), dma((S, g_parts)), dma((a_count,)), dma((S, parts_of)),
            dma((S, g_parts, C)), dma((S, g_parts, C)),
            dma((S, parts_of, E)), dma((S, parts_of, E)),
            dma((Q,)), dma((Q,)),
            dma((1,)), dma((1,)), dma((1,)), dma((1,)),
        ],
        compiler_params=pltpu.CompilerParams(
            collective_id=0, has_side_effects=True, vmem_limit_bytes=60 * 2**20),
        cost_estimate=pl.CostEstimate(
            flops=2 * local_rows * local_cols * (tokens + 2 * kept),
            bytes_accessed=2 * (local_rows + local_cols) * tokens, transcendentals=0),
        name="scores",
    )(activations, out_grads, words, keep_cols[None], row_start[None], row_step[None], val_sketch)


def solution(mesh):
    placed = (
        P("groups", ("sketch", "context"), None),
        P("groups", ("sketch", "example"), None),
        P(None, "context", None, "example", None),
        P(),
        P(("context", "example")),
        P(("context", "example")),
        P("sketch", ("context", "example")),
    )
    return jax.shard_map(
        body, mesh=mesh, in_specs=placed, out_specs=P(("groups", "sketch"), None), check_vma=False
    )
```

```python
import functools
import math

import jax
import jax.numpy as jnp
from jax import lax
from jax.experimental import pallas as pl
from jax.experimental.pallas import tpu as pltpu
from jax.sharding import PartitionSpec as P

MESH = pl.DeviceIdType.MESH
F32 = jnp.float32
BF16 = jnp.bfloat16
I32 = jnp.int32
LANES = 128
BITS = 16
ROWS = 256
WIDE = 512
WINDOW = 6


def log2(n):
    return n.bit_length() - 1


def sign_of(common):
    for shift in (16, 8, 4, 2, 1):
        common = jnp.bitwise_xor(common, jnp.right_shift(common, shift))
    return (1 - 2 * jnp.bitwise_and(common, 1)).astype(F32)


def iota(shape, axis):
    return lax.broadcasted_iota(I32, shape, axis)


def split(values):
    high = values.astype(BF16)
    return high, (values - high.astype(F32)).astype(BF16)


def place(s, c, k):
    return {"sketch": s, "context": c, "example": k}


def each(count, step):
    if count <= 16:
        for at in range(1, count):
            step(at)
    else:
        lax.fori_loop(1, count, lambda at, _: (step(at), 0)[1], 0)


def wrap(at, size):
    return jnp.bitwise_and(at, size - 1)


def kernel(sizes, scale, kr, act, grads, words_in, columns_in, begin_in, half_in, val_in, out,
           a_buf, g_buf, gp, gt, table, perm, hada, words, columns, begins, halves, val,
           part, turned, plain, ring, sketch, parts, sums,
           own_sem, gz_send, gz_recv, az_send, az_recv, gx_send, gx_recv, ax_send, ax_recv,
           r_send, r_recv, p_send, p_recv, s_send, s_recv):
    S, C, E = sizes
    Q = C * E
    s, c, k = lax.axis_index("sketch"), lax.axis_index("context"), lax.axis_index("example")
    me = c * E + k
    rp, gp_len = act.shape[1], grads.shape[1]
    gh = gp_len // C
    g_parts = 2 if gh % 64 == 0 else 1
    gq = gh // g_parts
    row_block = min(ROWS, rp)
    parts_of = rp // row_block
    ah = row_block // E
    total_rows, total_cols = a_buf.shape[0], g_buf.shape[0]
    in_width, out_width = total_rows * C, total_cols * E
    word_count = words.shape[1]
    kept = columns.shape[1]

    def member(m):
        m = jnp.int32(m)
        return wrap(s + jnp.right_shift(m, log2(Q)), S), wrap(me + m, Q)

    def spot(t, q):
        return place(t, jnp.right_shift(q, log2(E)), wrap(q, E))

    barrier = pltpu.get_barrier_semaphore()

    def greet(m):
        pl.semaphore_signal(barrier, inc=1, device_id=spot(*member(m)),
                            device_id_type=MESH)

    local = [
        pltpu.make_async_copy(src, dst, own_sem.at[at]) for at, (src, dst) in enumerate((
            (begin_in, begins), (half_in, halves), (columns_in, columns),
            (grads.at[s], g_buf.at[pl.ds(pl.multiple_of(s * gp_len, gp_len), gp_len)]),
            (act.at[s], a_buf.at[pl.ds(pl.multiple_of(s * rp, rp), rp)]),
            (words_in, words), (val_in, val)))
    ]
    each(S * Q, greet)
    for copy in local:
        copy.start()
    pl.semaphore_wait(barrier, S * Q - 1)

    def remote(src, dst, send, recv, target):
        return pltpu.make_async_remote_copy(
            src_ref=src, dst_ref=dst, send_sem=send, recv_sem=recv,
            device_id=target, device_id_type=MESH)

    g_count, a_count = (S - 1) * g_parts, (S - 1) * parts_of

    def g_rows(piece, h, part_at):
        return pl.ds(pl.multiple_of(piece * gp_len + part_at * gh + h * gq, gq), gq)

    def a_rows(piece, h, part_at):
        return pl.ds(pl.multiple_of(piece * rp + h * row_block + part_at * ah, ah), ah)

    def mate(n):
        far = S // 2 + jnp.right_shift(n, 1)
        near = jnp.right_shift(n + 1, 1)
        return jnp.bitwise_xor(s, jnp.where(jnp.bitwise_and(n, 1) == 0, far, near))

    def nth(n, parts_in):
        n = jnp.int32(n)
        return mate(jnp.right_shift(n, log2(parts_in))), wrap(n, parts_in)

    def g_send(n):
        t, h = nth(n, g_parts)
        return remote(grads.at[t, pl.ds(pl.multiple_of(c * gh + h * gq, gq), gq)],
                      g_buf.at[g_rows(s, h, c)], gz_send.at[n], gz_recv.at[s, h],
                      place(t, c, k))

    def a_send(n):
        t, h = nth(n, parts_of)
        return remote(act.at[t, pl.ds(pl.multiple_of(h * row_block + k * ah, ah), ah)],
                      a_buf.at[a_rows(s, h, k)], az_send.at[n], az_recv.at[s, h],
                      place(t, c, k))

    def g_pass(piece, h, m):
        rows = g_rows(piece, h, c)
        return remote(g_buf.at[rows], g_buf.at[rows], gx_send.at[piece, h, m],
                      gx_recv.at[piece, h, c], place(s, wrap(c + m, C), k))

    def a_pass(piece, h, m):
        rows = a_rows(piece, h, k)
        return remote(a_buf.at[rows], a_buf.at[rows], ax_send.at[piece, h, m],
                      ax_recv.at[piece, h, k], place(s, c, wrap(k + m, E)))

    def arrived(ref, sem):
        pltpu.make_async_copy(ref, ref, sem).wait()

    def pieces(step):
        each(S, lambda o: step(mate(jnp.int32(o - 1))))

    def issue(n):
        n = jnp.int32(n)

        @pl.when(n < g_count)
        def _():
            g_send(n).start()

        @pl.when(jnp.logical_and(n >= g_count, n < g_count + a_count))
        def _():
            a_send(n - g_count).start()

    lax.fori_loop(0, WINDOW, lambda n, _: (issue(n), 0)[1], 0)

    for copy in local[:2]:
        copy.wait()
    per_q = kept // Q
    ring[pl.ds(me, 1)] = jnp.zeros((1, 8, kept), I32)
    for q in range(Q):
        ring[me, 0:1, q * per_q:(q + 1) * per_q] = begins[...]
        ring[me, 1:2, q * per_q:(q + 1) * per_q] = halves[...]

    def r_copy(m):
        return remote(ring.at[me], ring.at[me], r_send.at[m], r_recv.at[me],
                      spot(s, wrap(me + m, Q)))

    each(Q, lambda m: r_copy(m).start())

    local[2].wait()
    width = out_width // kept
    kept_cols = columns[...] + iota((1, kept), 1) * width

    def tabulate(b, carry):
        at = iota((word_count, kept), 0) * BITS + b
        full = ((jnp.right_shift(at, log2(gp_len)) * E + k) * gp_len
                + jnp.bitwise_and(at, gp_len - 1))
        table[pl.ds(pl.multiple_of(b * word_count, word_count), word_count), :] = sign_of(
            jnp.bitwise_and(full, kept_cols)).astype(BF16)
        return carry

    lax.fori_loop(0, BITS, tabulate, 0)
    hada[...] = sign_of(jnp.bitwise_and(
        iota((row_block, row_block), 0), iota((row_block, row_block), 1))).astype(BF16)

    block = perm.shape[0]
    block_words = block // BITS
    blocks = total_cols // block
    row_at, col_at = iota((block, block), 0), iota((block, block), 1)
    source = (jnp.bitwise_and(row_at, block_words - 1) * BITS
              + jnp.right_shift(row_at, log2(block_words)))
    perm[...] = jnp.where(col_at == source, 1.0, 0.0).astype(BF16)

    def permute(at):
        rows = g_buf[pl.ds(pl.multiple_of(at * block, block), block), :]
        moved = jnp.dot(perm[...], rows, preferred_element_type=F32).astype(BF16)
        for b in range(BITS):
            gp[pl.ds(pl.multiple_of(b * word_count + at * block_words, block_words),
                     block_words), :] = moved[b * block_words:(b + 1) * block_words]

    piece_blocks = block == gp_len

    def g_whole(n):
        piece = mate(n)
        for h in range(g_parts):
            def wait(m):
                other = wrap(c + m, C)
                arrived(g_buf.at[g_rows(piece, h, other)], gx_recv.at[piece, h, other])
            each(C, wait)
        if piece_blocks:
            permute(piece)

    def g_step(n, carry):
        piece, h = nth(n, g_parts)
        arrived(g_buf.at[g_rows(piece, h, c)], gz_recv.at[piece, h])
        each(C, lambda m: g_pass(piece, h, m).start())
        issue(n + WINDOW)

        @pl.when(jnp.logical_and(h == 0, n > 0))
        def _():
            g_whole(jnp.right_shift(n, log2(g_parts)) - 1)
        return carry

    def r_arrived(m):
        q = wrap(me + m, Q)
        arrived(ring.at[q], r_recv.at[q])

    each(Q, r_arrived)
    lane = iota((1, kept), 1)
    begin = jnp.zeros((1, kept), I32)
    half = jnp.zeros((1, kept), I32)
    for q in range(Q):
        mine = jnp.right_shift(lane, log2(per_q)) == q
        begin = jnp.where(mine, ring[q, 0:1, :], begin)
        half = jnp.where(mine, ring[q, 1:2, :], half)
    fold = LANES // kr
    high_rows = kept // fold
    shape = (high_rows, LANES)
    wide_lane = iota(shape, 1)
    at_i = jnp.bitwise_and(wide_lane, kr - 1)
    group = jnp.right_shift(wide_lane, log2(kr))

    def down(vector):
        plain[...] = jnp.broadcast_to(vector, (kept, kept)).T
        got = plain[pl.ds(0, high_rows, stride=fold), :]
        for f in range(1, fold):
            got = jnp.where(group == f, plain[pl.ds(f, high_rows, stride=fold), :], got)
        return got

    row = jnp.bitwise_and(down(begin) + at_i * (2 * down(half) + 1), in_width - 1)
    piece_bits, context_bits = log2(rp), log2(C)
    sign = sign_of(jnp.bitwise_and(jnp.bitwise_and(jnp.right_shift(row, piece_bits), C - 1), c))
    held = (jnp.left_shift(jnp.right_shift(row, piece_bits + context_bits), piece_bits)
            + jnp.bitwise_and(row, rp - 1))
    in_block = jnp.bitwise_and(held, LANES - 1)
    which = jnp.right_shift(held, log2(LANES))
    local[3].wait()
    if piece_blocks:
        permute(s)
    lax.fori_loop(0, g_count, g_step, 0)
    g_whole(jnp.int32(S - 2))
    if not piece_blocks:
        lax.fori_loop(0, blocks, lambda at, _: (permute(at), 0)[1], 0)
    wide = min(WIDE, total_cols)

    def turn(at, carry):
        here = pl.ds(pl.multiple_of(at * wide, wide), wide)
        gt[:, here] = gp[here, :].T
        return carry

    lax.fori_loop(0, total_cols // wide, turn, 0)

    def score_rows(row):
        here = pl.ds(pl.multiple_of(row, row_block), row_block)
        a = a_buf[here, :]
        w = words[here, :]
        total = jnp.zeros((row_block, kept), F32)
        for at in range(total_cols // wide):
            grad = jnp.dot(a, gt[:, at * wide:(at + 1) * wide], preferred_element_type=F32)
            signed = []
            for bb in range(wide // word_count):
                bit = 1 << (at * (wide // word_count) + bb)
                one = grad[:, bb * word_count:(bb + 1) * word_count]
                signed.append(jnp.where(jnp.bitwise_and(w, bit) != 0, -one, one))
            high, low = split(jnp.concatenate(signed, axis=1))
            side = table[at * wide:(at + 1) * wide, :]
            total = total + jnp.dot(high, side, preferred_element_type=F32)
            total = total + jnp.dot(low, side, preferred_element_type=F32)
        got = jnp.dot(hada[...], jnp.concatenate(split(total), axis=1),
                      preferred_element_type=F32)
        part[here, :] = got[:, :kept] + got[:, kept:]

    local[4].wait()
    local[5].wait()

    def a_step(n, carry):
        piece, h = nth(n - parts_of, parts_of)
        n_next = n - parts_of + 1
        next_piece, h_next = nth(n_next, parts_of)

        @pl.when(jnp.logical_and(n_next >= 0, n_next < a_count))
        def _():
            arrived(a_buf.at[a_rows(next_piece, h_next, k)], az_recv.at[next_piece, h_next])
            each(E, lambda m: a_pass(next_piece, h_next, m).start())
            issue(g_count + n_next + WINDOW)

        @pl.when(n >= parts_of)
        def _():
            def wait(m):
                other = wrap(k + m, E)
                arrived(a_buf.at[a_rows(piece, h, other)], ax_recv.at[piece, h, other])
            each(E, wait)

        score_rows(piece * rp + h * row_block)
        return carry

    lax.fori_loop(0, S * parts_of, a_step, 0)

    mixed = [part[at:at + row_block, :] for at in range(0, total_rows, row_block)]
    step = 1
    while step < len(mixed):
        nxt = list(mixed)
        for at in range(len(mixed)):
            if at & step == 0:
                nxt[at] = mixed[at] + mixed[at + step]
                nxt[at + step] = mixed[at] - mixed[at + step]
        mixed = nxt
        step *= 2
    whole = mixed if row_block >= LANES else [
        jnp.concatenate(mixed[at:at + LANES // row_block], axis=0)
        for at in range(0, len(mixed), LANES // row_block)]
    turned_rows = 0
    for values in whole:
        for b in range(0, values.shape[0], LANES):
            turned[turned_rows:turned_rows + LANES, :] = values[b:b + LANES, :].T
            turned_rows += LANES

    picked = jnp.zeros(shape, F32)
    for at in range(total_rows // LANES):
        found = None
        for f in range(fold):
            values = turned[pl.ds(at * LANES + f, high_rows, stride=fold), :]
            got = jnp.take_along_axis(values, in_block, axis=1, mode="promise_in_bounds")
            found = got if found is None else jnp.where(group == f, got, found)
        picked = jnp.where(which == at, found, picked)
    sketch[...] = picked * sign * scale

    per = high_rows // Q
    mine_at = s * Q + me

    def q_rows(q):
        return pl.ds(pl.multiple_of(q * per, per), per)

    def p_copy(m):
        t, q = member(m)
        return remote(sketch.at[q_rows(q)], parts.at[mine_at], p_send.at[0], p_recv.at[0],
                      spot(t, q))

    each(S * Q, lambda m: p_copy(m).start())
    parts[pl.ds(mine_at, 1)] = sketch[q_rows(me), :][None]
    local[6].wait()

    def sent(piece):
        for h in range(g_parts):
            each(C, lambda m: g_pass(piece, h, m).wait_send())
        for h in range(parts_of):
            each(E, lambda m: a_pass(piece, h, m).wait_send())

    pieces(sent)
    each(g_count + 1, lambda n: g_send(n - 1).wait_send())
    each(a_count + 1, lambda n: a_send(n - 1).wait_send())
    each(Q, lambda m: r_copy(m).wait_send())
    others = pl.ds(0, S * Q - 1)
    arrived(parts.at[others], p_recv.at[0])
    nvl = val.shape[0]
    nv = nvl * S
    out_lane = iota((1, LANES), 1)

    def products(e):
        own = parts[e * Q]
        for q in range(1, Q):
            own = own + parts[e * Q + q]
        total = jnp.zeros((nvl, LANES), F32)
        for r in range(per):
            total = total + val[:, r * LANES:(r + 1) * LANES] * own[r:r + 1, :]
        squares = jnp.sum(own * own, axis=0, keepdims=True)
        tall = jnp.concatenate(
            [total, squares, jnp.zeros((LANES - nvl - 1, LANES), F32)], axis=0)
        line = jnp.sum(tall.T, axis=0, keepdims=True)
        norm = jnp.sum(squares, axis=1, keepdims=True)
        mine = pltpu.roll(jnp.where(out_lane < nvl, line, 0.0), s * nvl, axis=1)
        mine = jnp.where(out_lane == nv, norm * (s == 0).astype(F32), mine)
        return jnp.broadcast_to(mine, (8, LANES))

    answers = part

    def e_rows(e):
        return pl.ds(pl.multiple_of(e * 8, 8), 8)

    def put(e, carry):
        answers[e_rows(e), :] = products(e)
        return carry

    lax.fori_loop(0, S, put, 0)

    def s_copy(m):
        t, q = member(m)
        return remote(answers.at[e_rows(t)], sums.at[mine_at], s_send.at[0], s_recv.at[0],
                      spot(t, q))

    each(S * Q, lambda m: s_copy(m).start())
    sums[pl.ds(mine_at, 1)] = answers[e_rows(s), :][None]

    arrived(sums.at[others], s_recv.at[0])
    all_sums = sums[0]
    for at in range(1, S * Q):
        all_sums = all_sums + sums[at]
    out[...] = all_sums[0:1, :nv] / jnp.sqrt(all_sums[0:1, nv:nv + 1] + 1e-06)
    arrived(parts.at[others], p_send.at[0])
    arrived(sums.at[others], s_send.at[0])


def body(activations, out_grads, sign_bits, keep_cols, row_start, row_step, val_sketch):
    S, C, E = lax.axis_size("sketch"), lax.axis_size("context"), lax.axis_size("example")
    Q = C * E
    rp, tokens = activations.shape[1:]
    gp_len = out_grads.shape[1]
    local_rows, local_cols = S * rp, S * gp_len
    in_width, out_width = local_rows * C, local_cols * E
    kept = keep_cols.shape[0]
    keep = val_sketch.shape[1] * Q
    kr = keep // kept
    nv = val_sketch.shape[0] * S
    words = sign_bits.reshape(local_rows, -1)
    row_block = min(ROWS, rp)
    parts_of = rp // row_block
    a_count = (S - 1) * parts_of
    g_parts = 2 if (gp_len // C) % 64 == 0 else 1
    g_count = (S - 1) * g_parts
    hbm = pl.BlockSpec(memory_space=pl.ANY)
    dma = pltpu.SemaphoreType.DMA
    block = min(WIDE, local_cols)
    return pl.pallas_call(
        functools.partial(
            kernel, (S, C, E), 1.0 / (math.sqrt(in_width) * math.sqrt(out_width)), kr),
        out_shape=jax.ShapeDtypeStruct((1, nv), F32),
        in_specs=[hbm] * 7,
        out_specs=pl.BlockSpec(memory_space=pltpu.VMEM),
        scratch_shapes=[
            pltpu.VMEM((local_rows, tokens), BF16),
            pltpu.VMEM((local_cols, tokens), BF16),
            pltpu.VMEM((local_cols, tokens), BF16),
            pltpu.VMEM((tokens, local_cols), BF16),
            pltpu.VMEM((local_cols, kept), BF16),
            pltpu.VMEM((block, block), BF16),
            pltpu.VMEM((row_block, row_block), BF16),
            pltpu.VMEM(words.shape, I32),
            pltpu.VMEM((1, kept), I32),
            pltpu.VMEM((1, kept // Q), I32),
            pltpu.VMEM((1, kept // Q), I32),
            pltpu.VMEM(val_sketch.shape, F32),
            pltpu.VMEM((local_rows, kept), F32),
            pltpu.VMEM((local_rows, LANES), F32),
            pltpu.VMEM((kept, kept), I32),
            pltpu.VMEM((Q, 8, kept), I32),
            pltpu.VMEM((keep // LANES, LANES), F32),
            pltpu.VMEM((S * Q, keep // LANES // Q, LANES), F32),
            pltpu.VMEM((S * Q, 8, LANES), F32),
            dma((7,)),
            dma((g_count,)), dma((S, g_parts)), dma((a_count,)), dma((S, parts_of)),
            dma((S, g_parts, C)), dma((S, g_parts, C)),
            dma((S, parts_of, E)), dma((S, parts_of, E)),
            dma((Q,)), dma((Q,)),
            dma((1,)), dma((1,)), dma((1,)), dma((1,)),
        ],
        compiler_params=pltpu.CompilerParams(
            collective_id=0, has_side_effects=True, vmem_limit_bytes=60 * 2**20),
        cost_estimate=pl.CostEstimate(
            flops=2 * local_rows * local_cols * (tokens + 2 * kept),
            bytes_accessed=2 * (local_rows + local_cols) * tokens, transcendentals=0),
        name="scores",
    )(activations, out_grads, words, keep_cols[None], row_start[None], row_step[None], val_sketch)


def solution(mesh):
    placed = (
        P("groups", ("sketch", "context"), None),
        P("groups", ("sketch", "example"), None),
        P(None, "context", None, "example", None),
        P(),
        P(("context", "example")),
        P(("context", "example")),
        P("sketch", ("context", "example")),
    )
    return jax.shard_map(
        body, mesh=mesh, in_specs=placed, out_specs=P(("groups", "sketch"), None), check_vma=False
    )
```

```python
import functools
import math

import jax
import jax.numpy as jnp
from jax import lax
from jax.experimental import pallas as pl
from jax.experimental.pallas import tpu as pltpu
from jax.sharding import PartitionSpec as P

MESH = pl.DeviceIdType.MESH
F32 = jnp.float32
BF16 = jnp.bfloat16
I32 = jnp.int32
LANES = 128
BITS = 16
ROWS = 256
WIDE = 512
WINDOW = 6


def log2(n):
    return n.bit_length() - 1


def sign_of(common):
    for shift in (16, 8, 4, 2, 1):
        common = jnp.bitwise_xor(common, jnp.right_shift(common, shift))
    return (1 - 2 * jnp.bitwise_and(common, 1)).astype(F32)


def iota(shape, axis):
    return lax.broadcasted_iota(I32, shape, axis)


def split(values):
    high = values.astype(BF16)
    return high, (values - high.astype(F32)).astype(BF16)


def place(s, c, k):
    return {"sketch": s, "context": c, "example": k}


def each(count, step):
    if count <= 16:
        for at in range(1, count):
            step(at)
    else:
        lax.fori_loop(1, count, lambda at, _: (step(at), 0)[1], 0)


def wrap(at, size):
    return jnp.bitwise_and(at, size - 1)


def kernel(sizes, scale, kr, act, grads, words_in, columns_in, begin_in, half_in, val_in, out,
           a_buf, g_buf, gp, gt, table, perm, hada, signs, words, columns, begins, halves, val,
           part, turned, plain, ring, sketch, parts, sums,
           own_sem, gz_send, gz_recv, az_send, az_recv, gx_send, gx_recv, ax_send, ax_recv,
           r_send, r_recv, p_send, p_recv, s_send, s_recv):
    S, C, E = sizes
    Q = C * E
    s, c, k = lax.axis_index("sketch"), lax.axis_index("context"), lax.axis_index("example")
    me = c * E + k
    rp, gp_len = act.shape[1], grads.shape[1]
    gh = gp_len // C
    g_parts = 2 if gh % 64 == 0 else 1
    gq = gh // g_parts
    row_block = min(ROWS, rp)
    parts_of = rp // row_block
    ah = row_block // E
    total_rows, total_cols = a_buf.shape[0], g_buf.shape[0]
    in_width, out_width = total_rows * C, total_cols * E
    word_count = words.shape[1]
    kept = columns.shape[1]

    def member(m):
        m = jnp.int32(m)
        return wrap(s + jnp.right_shift(m, log2(Q)), S), wrap(me + m, Q)

    def spot(t, q):
        return place(t, jnp.right_shift(q, log2(E)), wrap(q, E))

    barrier = pltpu.get_barrier_semaphore()

    def greet(m):
        pl.semaphore_signal(barrier, inc=1, device_id=spot(*member(m)),
                            device_id_type=MESH)

    local = [
        pltpu.make_async_copy(src, dst, own_sem.at[at]) for at, (src, dst) in enumerate((
            (begin_in, begins), (half_in, halves), (columns_in, columns),
            (grads.at[s], g_buf.at[pl.ds(pl.multiple_of(s * gp_len, gp_len), gp_len)]),
            (act.at[s], a_buf.at[pl.ds(pl.multiple_of(s * rp, rp), rp)]),
            (words_in, words), (val_in, val)))
    ]
    each(S * Q, greet)
    for copy in local:
        copy.start()
    pl.semaphore_wait(barrier, S * Q - 1)

    def remote(src, dst, send, recv, target):
        return pltpu.make_async_remote_copy(
            src_ref=src, dst_ref=dst, send_sem=send, recv_sem=recv,
            device_id=target, device_id_type=MESH)

    g_count, a_count = (S - 1) * g_parts, (S - 1) * parts_of

    def g_rows(piece, h, part_at):
        return pl.ds(pl.multiple_of(piece * gp_len + part_at * gh + h * gq, gq), gq)

    def a_rows(piece, h, part_at):
        return pl.ds(pl.multiple_of(piece * rp + h * row_block + part_at * ah, ah), ah)

    def mate(n):
        far = S // 2 + jnp.right_shift(n, 1)
        near = jnp.right_shift(n + 1, 1)
        return jnp.bitwise_xor(s, jnp.where(jnp.bitwise_and(n, 1) == 0, far, near))

    def nth(n, parts_in):
        n = jnp.int32(n)
        return mate(jnp.right_shift(n, log2(parts_in))), wrap(n, parts_in)

    def g_send(n):
        t, h = nth(n, g_parts)
        return remote(grads.at[t, pl.ds(pl.multiple_of(c * gh + h * gq, gq), gq)],
                      g_buf.at[g_rows(s, h, c)], gz_send.at[n], gz_recv.at[s, h],
                      place(t, c, k))

    def a_send(n):
        t, h = nth(n, parts_of)
        return remote(act.at[t, pl.ds(pl.multiple_of(h * row_block + k * ah, ah), ah)],
                      a_buf.at[a_rows(s, h, k)], az_send.at[n], az_recv.at[s, h],
                      place(t, c, k))

    def g_pass(piece, h, m):
        rows = g_rows(piece, h, c)
        return remote(g_buf.at[rows], g_buf.at[rows], gx_send.at[piece, h, m],
                      gx_recv.at[piece, h, c], place(s, wrap(c + m, C), k))

    def a_pass(piece, h, m):
        rows = a_rows(piece, h, k)
        return remote(a_buf.at[rows], a_buf.at[rows], ax_send.at[piece, h, m],
                      ax_recv.at[piece, h, k], place(s, c, wrap(k + m, E)))

    def arrived(ref, sem):
        pltpu.make_async_copy(ref, ref, sem).wait()

    def pieces(step):
        each(S, lambda o: step(mate(jnp.int32(o - 1))))

    def issue(n):
        n = jnp.int32(n)

        @pl.when(n < g_count)
        def _():
            g_send(n).start()

        @pl.when(jnp.logical_and(n >= g_count, n < g_count + a_count))
        def _():
            a_send(n - g_count).start()

    lax.fori_loop(0, WINDOW, lambda n, _: (issue(n), 0)[1], 0)

    for copy in local[:2]:
        copy.wait()
    per_q = kept // Q
    ring[pl.ds(me, 1)] = jnp.zeros((1, 8, kept), I32)
    for q in range(Q):
        ring[me, 0:1, q * per_q:(q + 1) * per_q] = begins[...]
        ring[me, 1:2, q * per_q:(q + 1) * per_q] = halves[...]

    def r_copy(m):
        return remote(ring.at[me], ring.at[me], r_send.at[m], r_recv.at[me],
                      spot(s, wrap(me + m, Q)))

    each(Q, lambda m: r_copy(m).start())

    local[2].wait()
    width = out_width // kept
    kept_cols = columns[...] + iota((1, kept), 1) * width

    def tabulate(b, carry):
        at = iota((word_count, kept), 0) * BITS + b
        full = ((jnp.right_shift(at, log2(gp_len)) * E + k) * gp_len
                + jnp.bitwise_and(at, gp_len - 1))
        table[pl.ds(pl.multiple_of(b * word_count, word_count), word_count), :] = sign_of(
            jnp.bitwise_and(full, kept_cols)).astype(BF16)
        return carry

    lax.fori_loop(0, BITS, tabulate, 0)
    hada[...] = sign_of(jnp.bitwise_and(
        iota((row_block, row_block), 0), iota((row_block, row_block), 1))).astype(BF16)

    block = perm.shape[0]
    block_words = block // BITS
    blocks = total_cols // block
    row_at, col_at = iota((block, block), 0), iota((block, block), 1)
    source = (jnp.bitwise_and(row_at, block_words - 1) * BITS
              + jnp.right_shift(row_at, log2(block_words)))
    perm[...] = jnp.where(col_at == source, 1.0, 0.0).astype(BF16)

    def permute(at):
        rows = g_buf[pl.ds(pl.multiple_of(at * block, block), block), :]
        moved = jnp.dot(perm[...], rows, preferred_element_type=F32).astype(BF16)
        for b in range(BITS):
            gp[pl.ds(pl.multiple_of(b * word_count + at * block_words, block_words),
                     block_words), :] = moved[b * block_words:(b + 1) * block_words]

    piece_blocks = block == gp_len

    def g_whole(n):
        piece = mate(n)
        for h in range(g_parts):
            def wait(m):
                other = wrap(c + m, C)
                arrived(g_buf.at[g_rows(piece, h, other)], gx_recv.at[piece, h, other])
            each(C, wait)
        if piece_blocks:
            permute(piece)

    def g_step(n, carry):
        piece, h = nth(n, g_parts)
        arrived(g_buf.at[g_rows(piece, h, c)], gz_recv.at[piece, h])
        each(C, lambda m: g_pass(piece, h, m).start())
        issue(n + WINDOW)

        @pl.when(jnp.logical_and(h == 0, n > 0))
        def _():
            g_whole(jnp.right_shift(n, log2(g_parts)) - 1)
        return carry

    def r_arrived(m):
        q = wrap(me + m, Q)
        arrived(ring.at[q], r_recv.at[q])

    each(Q, r_arrived)
    lane = iota((1, kept), 1)
    begin = jnp.zeros((1, kept), I32)
    half = jnp.zeros((1, kept), I32)
    for q in range(Q):
        mine = jnp.right_shift(lane, log2(per_q)) == q
        begin = jnp.where(mine, ring[q, 0:1, :], begin)
        half = jnp.where(mine, ring[q, 1:2, :], half)
    fold = LANES // kr
    high_rows = kept // fold
    shape = (high_rows, LANES)
    wide_lane = iota(shape, 1)
    at_i = jnp.bitwise_and(wide_lane, kr - 1)
    group = jnp.right_shift(wide_lane, log2(kr))

    def down(vector):
        plain[...] = jnp.broadcast_to(vector, (kept, kept)).T
        got = plain[pl.ds(0, high_rows, stride=fold), :]
        for f in range(1, fold):
            got = jnp.where(group == f, plain[pl.ds(f, high_rows, stride=fold), :], got)
        return got

    row = jnp.bitwise_and(down(begin) + at_i * (2 * down(half) + 1), in_width - 1)
    piece_bits, context_bits = log2(rp), log2(C)
    sign = sign_of(jnp.bitwise_and(jnp.bitwise_and(jnp.right_shift(row, piece_bits), C - 1), c))
    held = (jnp.left_shift(jnp.right_shift(row, piece_bits + context_bits), piece_bits)
            + jnp.bitwise_and(row, rp - 1))
    in_block = jnp.bitwise_and(held, LANES - 1)
    which = jnp.right_shift(held, log2(LANES))
    local[5].wait()

    def expand(at, carry):
        here = pl.ds(pl.multiple_of(at * row_block, row_block), row_block)
        w = words[here, :]
        for b in range(BITS):
            signs[here, b * word_count:(b + 1) * word_count] = jnp.where(
                jnp.bitwise_and(w, 1 << b) != 0, -1.0, 1.0).astype(BF16)
        return carry

    lax.fori_loop(0, total_rows // row_block, expand, 0)
    local[3].wait()
    if piece_blocks:
        permute(s)
    lax.fori_loop(0, g_count, g_step, 0)
    g_whole(jnp.int32(S - 2))
    if not piece_blocks:
        lax.fori_loop(0, blocks, lambda at, _: (permute(at), 0)[1], 0)
    wide = min(WIDE, total_cols)

    def turn(at, carry):
        here = pl.ds(pl.multiple_of(at * wide, wide), wide)
        gt[:, here] = gp[here, :].T
        return carry

    lax.fori_loop(0, total_cols // wide, turn, 0)

    def score_rows(row):
        here = pl.ds(pl.multiple_of(row, row_block), row_block)
        a = a_buf[here, :]
        total = jnp.zeros((row_block, kept), F32)
        for at in range(total_cols // wide):
            grad = jnp.dot(a, gt[:, at * wide:(at + 1) * wide], preferred_element_type=F32)
            high, low = split(grad)
            sign_here = signs[here, at * wide:(at + 1) * wide]
            high, low = high * sign_here, low * sign_here
            side = table[at * wide:(at + 1) * wide, :]
            total = total + jnp.dot(high, side, preferred_element_type=F32)
            total = total + jnp.dot(low, side, preferred_element_type=F32)
        got = jnp.dot(hada[...], jnp.concatenate(split(total), axis=1),
                      preferred_element_type=F32)
        part[here, :] = got[:, :kept] + got[:, kept:]

    local[4].wait()

    def a_step(n, carry):
        piece, h = nth(n - parts_of, parts_of)
        n_next = n - parts_of + 1
        next_piece, h_next = nth(n_next, parts_of)

        @pl.when(jnp.logical_and(n_next >= 0, n_next < a_count))
        def _():
            arrived(a_buf.at[a_rows(next_piece, h_next, k)], az_recv.at[next_piece, h_next])
            each(E, lambda m: a_pass(next_piece, h_next, m).start())
            issue(g_count + n_next + WINDOW)

        @pl.when(n >= parts_of)
        def _():
            def wait(m):
                other = wrap(k + m, E)
                arrived(a_buf.at[a_rows(piece, h, other)], ax_recv.at[piece, h, other])
            each(E, wait)

        score_rows(piece * rp + h * row_block)
        return carry

    lax.fori_loop(0, S * parts_of, a_step, 0)

    mixed = [part[at:at + row_block, :] for at in range(0, total_rows, row_block)]
    step = 1
    while step < len(mixed):
        nxt = list(mixed)
        for at in range(len(mixed)):
            if at & step == 0:
                nxt[at] = mixed[at] + mixed[at + step]
                nxt[at + step] = mixed[at] - mixed[at + step]
        mixed = nxt
        step *= 2
    whole = mixed if row_block >= LANES else [
        jnp.concatenate(mixed[at:at + LANES // row_block], axis=0)
        for at in range(0, len(mixed), LANES // row_block)]
    turned_rows = 0
    for values in whole:
        for b in range(0, values.shape[0], LANES):
            turned[turned_rows:turned_rows + LANES, :] = values[b:b + LANES, :].T
            turned_rows += LANES

    picked = jnp.zeros(shape, F32)
    for at in range(total_rows // LANES):
        found = None
        for f in range(fold):
            values = turned[pl.ds(at * LANES + f, high_rows, stride=fold), :]
            got = jnp.take_along_axis(values, in_block, axis=1, mode="promise_in_bounds")
            found = got if found is None else jnp.where(group == f, got, found)
        picked = jnp.where(which == at, found, picked)
    sketch[...] = picked * sign * scale

    per = high_rows // Q
    mine_at = s * Q + me

    def q_rows(q):
        return pl.ds(pl.multiple_of(q * per, per), per)

    def p_copy(m):
        t, q = member(m)
        return remote(sketch.at[q_rows(q)], parts.at[mine_at], p_send.at[0], p_recv.at[0],
                      spot(t, q))

    each(S * Q, lambda m: p_copy(m).start())
    parts[pl.ds(mine_at, 1)] = sketch[q_rows(me), :][None]
    local[6].wait()

    def sent(piece):
        for h in range(g_parts):
            each(C, lambda m: g_pass(piece, h, m).wait_send())
        for h in range(parts_of):
            each(E, lambda m: a_pass(piece, h, m).wait_send())

    pieces(sent)
    each(g_count + 1, lambda n: g_send(n - 1).wait_send())
    each(a_count + 1, lambda n: a_send(n - 1).wait_send())
    each(Q, lambda m: r_copy(m).wait_send())
    others = pl.ds(0, S * Q - 1)
    arrived(parts.at[others], p_recv.at[0])
    nvl = val.shape[0]
    nv = nvl * S
    out_lane = iota((1, LANES), 1)

    def products(e):
        own = parts[e * Q]
        for q in range(1, Q):
            own = own + parts[e * Q + q]
        total = jnp.zeros((nvl, LANES), F32)
        for r in range(per):
            total = total + val[:, r * LANES:(r + 1) * LANES] * own[r:r + 1, :]
        squares = jnp.sum(own * own, axis=0, keepdims=True)
        tall = jnp.concatenate(
            [total, squares, jnp.zeros((LANES - nvl - 1, LANES), F32)], axis=0)
        line = jnp.sum(tall.T, axis=0, keepdims=True)
        norm = jnp.sum(squares, axis=1, keepdims=True)
        mine = pltpu.roll(jnp.where(out_lane < nvl, line, 0.0), s * nvl, axis=1)
        mine = jnp.where(out_lane == nv, norm * (s == 0).astype(F32), mine)
        return jnp.broadcast_to(mine, (8, LANES))

    answers = part

    def e_rows(e):
        return pl.ds(pl.multiple_of(e * 8, 8), 8)

    def put(e, carry):
        answers[e_rows(e), :] = products(e)
        return carry

    lax.fori_loop(0, S, put, 0)

    def s_copy(m):
        t, q = member(m)
        return remote(answers.at[e_rows(t)], sums.at[mine_at], s_send.at[0], s_recv.at[0],
                      spot(t, q))

    each(S * Q, lambda m: s_copy(m).start())
    sums[pl.ds(mine_at, 1)] = answers[e_rows(s), :][None]

    arrived(sums.at[others], s_recv.at[0])
    all_sums = sums[0]
    for at in range(1, S * Q):
        all_sums = all_sums + sums[at]
    out[...] = all_sums[0:1, :nv] / jnp.sqrt(all_sums[0:1, nv:nv + 1] + 1e-06)
    arrived(parts.at[others], p_send.at[0])
    arrived(sums.at[others], s_send.at[0])


def body(activations, out_grads, sign_bits, keep_cols, row_start, row_step, val_sketch):
    S, C, E = lax.axis_size("sketch"), lax.axis_size("context"), lax.axis_size("example")
    Q = C * E
    rp, tokens = activations.shape[1:]
    gp_len = out_grads.shape[1]
    local_rows, local_cols = S * rp, S * gp_len
    in_width, out_width = local_rows * C, local_cols * E
    kept = keep_cols.shape[0]
    keep = val_sketch.shape[1] * Q
    kr = keep // kept
    nv = val_sketch.shape[0] * S
    words = sign_bits.reshape(local_rows, -1)
    row_block = min(ROWS, rp)
    parts_of = rp // row_block
    a_count = (S - 1) * parts_of
    g_parts = 2 if (gp_len // C) % 64 == 0 else 1
    g_count = (S - 1) * g_parts
    hbm = pl.BlockSpec(memory_space=pl.ANY)
    dma = pltpu.SemaphoreType.DMA
    block = min(WIDE, local_cols)
    return pl.pallas_call(
        functools.partial(
            kernel, (S, C, E), 1.0 / (math.sqrt(in_width) * math.sqrt(out_width)), kr),
        out_shape=jax.ShapeDtypeStruct((1, nv), F32),
        in_specs=[hbm] * 7,
        out_specs=pl.BlockSpec(memory_space=pltpu.VMEM),
        scratch_shapes=[
            pltpu.VMEM((local_rows, tokens), BF16),
            pltpu.VMEM((local_cols, tokens), BF16),
            pltpu.VMEM((local_cols, tokens), BF16),
            pltpu.VMEM((tokens, local_cols), BF16),
            pltpu.VMEM((local_cols, kept), BF16),
            pltpu.VMEM((block, block), BF16),
            pltpu.VMEM((row_block, row_block), BF16),
            pltpu.VMEM((local_rows, local_cols), BF16),
            pltpu.VMEM(words.shape, I32),
            pltpu.VMEM((1, kept), I32),
            pltpu.VMEM((1, kept // Q), I32),
            pltpu.VMEM((1, kept // Q), I32),
            pltpu.VMEM(val_sketch.shape, F32),
            pltpu.VMEM((local_rows, kept), F32),
            pltpu.VMEM((local_rows, LANES), F32),
            pltpu.VMEM((kept, kept), I32),
            pltpu.VMEM((Q, 8, kept), I32),
            pltpu.VMEM((keep // LANES, LANES), F32),
            pltpu.VMEM((S * Q, keep // LANES // Q, LANES), F32),
            pltpu.VMEM((S * Q, 8, LANES), F32),
            dma((7,)),
            dma((g_count,)), dma((S, g_parts)), dma((a_count,)), dma((S, parts_of)),
            dma((S, g_parts, C)), dma((S, g_parts, C)),
            dma((S, parts_of, E)), dma((S, parts_of, E)),
            dma((Q,)), dma((Q,)),
            dma((1,)), dma((1,)), dma((1,)), dma((1,)),
        ],
        compiler_params=pltpu.CompilerParams(
            collective_id=0, has_side_effects=True, vmem_limit_bytes=60 * 2**20),
        cost_estimate=pl.CostEstimate(
            flops=2 * local_rows * local_cols * (tokens + 2 * kept),
            bytes_accessed=2 * (local_rows + local_cols) * tokens, transcendentals=0),
        name="scores",
    )(activations, out_grads, words, keep_cols[None], row_start[None], row_step[None], val_sketch)


def solution(mesh):
    placed = (
        P("groups", ("sketch", "context"), None),
        P("groups", ("sketch", "example"), None),
        P(None, "context", None, "example", None),
        P(),
        P(("context", "example")),
        P(("context", "example")),
        P("sketch", ("context", "example")),
    )
    return jax.shard_map(
        body, mesh=mesh, in_specs=placed, out_specs=P(("groups", "sketch"), None), check_vma=False
    )
```

```python
import functools
import math

import jax
import jax.numpy as jnp
from jax import lax
from jax.experimental import pallas as pl
from jax.experimental.pallas import tpu as pltpu
from jax.sharding import PartitionSpec as P

MESH = pl.DeviceIdType.MESH
F32 = jnp.float32
BF16 = jnp.bfloat16
I32 = jnp.int32
LANES = 128
BITS = 16
ROWS = 256
WIDE = 512
WINDOW = 6


def log2(n):
    return n.bit_length() - 1


def sign_of(common):
    for shift in (16, 8, 4, 2, 1):
        common = jnp.bitwise_xor(common, jnp.right_shift(common, shift))
    return (1 - 2 * jnp.bitwise_and(common, 1)).astype(F32)


def iota(shape, axis):
    return lax.broadcasted_iota(I32, shape, axis)


def split(values):
    high = values.astype(BF16)
    return high, (values - high.astype(F32)).astype(BF16)


def place(s, c, k):
    return {"sketch": s, "context": c, "example": k}


def each(count, step):
    if count <= 16:
        for at in range(1, count):
            step(at)
    else:
        lax.fori_loop(1, count, lambda at, _: (step(at), 0)[1], 0)


def wrap(at, size):
    return jnp.bitwise_and(at, size - 1)


def kernel(sizes, scale, kr, act, grads, words_in, columns_in, begin_in, half_in, val_in, out,
           a_buf, g_buf, gp, gt, table, perm, hada, signs, words, columns, begins, halves, val,
           turned, plain, ring, sketch, parts, sums,
           own_sem, gz_send, gz_recv, az_send, az_recv, gx_send, gx_recv, ax_send, ax_recv,
           r_send, r_recv, p_send, p_recv, s_send, s_recv):
    S, C, E = sizes
    Q = C * E
    s, c, k = lax.axis_index("sketch"), lax.axis_index("context"), lax.axis_index("example")
    me = c * E + k
    rp, gp_len = act.shape[1], grads.shape[1]
    gh = gp_len // C
    g_parts = 2 if gh % 64 == 0 else 1
    gq = gh // g_parts
    row_block = min(ROWS, rp)
    parts_of = rp // row_block
    ah = row_block // E
    total_rows, total_cols = a_buf.shape[0], g_buf.shape[0]
    in_width, out_width = total_rows * C, total_cols * E
    word_count = words.shape[1]
    kept = columns.shape[1]

    def member(m):
        m = jnp.int32(m)
        return wrap(s + jnp.right_shift(m, log2(Q)), S), wrap(me + m, Q)

    def spot(t, q):
        return place(t, jnp.right_shift(q, log2(E)), wrap(q, E))

    barrier = pltpu.get_barrier_semaphore()

    def greet(m):
        pl.semaphore_signal(barrier, inc=1, device_id=spot(*member(m)),
                            device_id_type=MESH)

    local = [
        pltpu.make_async_copy(src, dst, own_sem.at[at]) for at, (src, dst) in enumerate((
            (begin_in, begins), (half_in, halves), (columns_in, columns),
            (grads.at[s], g_buf.at[pl.ds(pl.multiple_of(s * gp_len, gp_len), gp_len)]),
            (act.at[s], a_buf.at[pl.ds(pl.multiple_of(s * rp, rp), rp)]),
            (words_in, words), (val_in, val)))
    ]
    each(S * Q, greet)
    for copy in local:
        copy.start()
    pl.semaphore_wait(barrier, S * Q - 1)

    def remote(src, dst, send, recv, target):
        return pltpu.make_async_remote_copy(
            src_ref=src, dst_ref=dst, send_sem=send, recv_sem=recv,
            device_id=target, device_id_type=MESH)

    g_count, a_count = (S - 1) * g_parts, (S - 1) * parts_of

    def g_rows(piece, h, part_at):
        return pl.ds(pl.multiple_of(piece * gp_len + part_at * gh + h * gq, gq), gq)

    def a_rows(piece, h, part_at):
        return pl.ds(pl.multiple_of(piece * rp + h * row_block + part_at * ah, ah), ah)

    def mate(n):
        far = S // 2 + jnp.right_shift(n, 1)
        near = jnp.right_shift(n + 1, 1)
        return jnp.bitwise_xor(s, jnp.where(jnp.bitwise_and(n, 1) == 0, far, near))

    def nth(n, parts_in):
        n = jnp.int32(n)
        return mate(jnp.right_shift(n, log2(parts_in))), wrap(n, parts_in)

    def g_send(n):
        t, h = nth(n, g_parts)
        return remote(grads.at[t, pl.ds(pl.multiple_of(c * gh + h * gq, gq), gq)],
                      g_buf.at[g_rows(s, h, c)], gz_send.at[n], gz_recv.at[s, h],
                      place(t, c, k))

    def a_send(n):
        t, h = nth(n, parts_of)
        return remote(act.at[t, pl.ds(pl.multiple_of(h * row_block + k * ah, ah), ah)],
                      a_buf.at[a_rows(s, h, k)], az_send.at[n], az_recv.at[s, h],
                      place(t, c, k))

    def g_pass(piece, h, m):
        rows = g_rows(piece, h, c)
        return remote(g_buf.at[rows], g_buf.at[rows], gx_send.at[piece, h, m],
                      gx_recv.at[piece, h, c], place(s, wrap(c + m, C), k))

    def a_pass(piece, h, m):
        rows = a_rows(piece, h, k)
        return remote(a_buf.at[rows], a_buf.at[rows], ax_send.at[piece, h, m],
                      ax_recv.at[piece, h, k], place(s, c, wrap(k + m, E)))

    def arrived(ref, sem):
        pltpu.make_async_copy(ref, ref, sem).wait()

    def pieces(step):
        each(S, lambda o: step(mate(jnp.int32(o - 1))))

    def issue(n):
        n = jnp.int32(n)

        @pl.when(n < g_count)
        def _():
            g_send(n).start()

        @pl.when(jnp.logical_and(n >= g_count, n < g_count + a_count))
        def _():
            a_send(n - g_count).start()

    lax.fori_loop(0, WINDOW, lambda n, _: (issue(n), 0)[1], 0)

    for copy in local[:2]:
        copy.wait()
    per_q = kept // Q
    ring[pl.ds(me, 1)] = jnp.zeros((1, 8, kept), I32)
    for q in range(Q):
        ring[me, 0:1, q * per_q:(q + 1) * per_q] = begins[...]
        ring[me, 1:2, q * per_q:(q + 1) * per_q] = halves[...]

    def r_copy(m):
        return remote(ring.at[me], ring.at[me], r_send.at[m], r_recv.at[me],
                      spot(s, wrap(me + m, Q)))

    each(Q, lambda m: r_copy(m).start())

    local[2].wait()
    width = out_width // kept
    kept_cols = columns[...] + iota((1, kept), 1) * width

    def tabulate(b, carry):
        at = iota((word_count, kept), 0) * BITS + b
        full = ((jnp.right_shift(at, log2(gp_len)) * E + k) * gp_len
                + jnp.bitwise_and(at, gp_len - 1))
        table[pl.ds(pl.multiple_of(b * word_count, word_count), word_count), :] = sign_of(
            jnp.bitwise_and(full, kept_cols)).astype(BF16)
        return carry

    lax.fori_loop(0, BITS, tabulate, 0)
    hada[...] = sign_of(jnp.bitwise_and(
        iota((row_block, row_block), 0), iota((row_block, row_block), 1))).astype(BF16)

    block = perm.shape[0]
    block_words = block // BITS
    blocks = total_cols // block
    row_at, col_at = iota((block, block), 0), iota((block, block), 1)
    source = (jnp.bitwise_and(row_at, block_words - 1) * BITS
              + jnp.right_shift(row_at, log2(block_words)))
    perm[...] = jnp.where(col_at == source, 1.0, 0.0).astype(BF16)

    def permute(at):
        rows = g_buf[pl.ds(pl.multiple_of(at * block, block), block), :]
        moved = jnp.dot(perm[...], rows, preferred_element_type=F32).astype(BF16)
        for b in range(BITS):
            gp[pl.ds(pl.multiple_of(b * word_count + at * block_words, block_words),
                     block_words), :] = moved[b * block_words:(b + 1) * block_words]

    piece_blocks = block == gp_len

    def g_whole(n):
        piece = mate(n)
        for h in range(g_parts):
            def wait(m):
                other = wrap(c + m, C)
                arrived(g_buf.at[g_rows(piece, h, other)], gx_recv.at[piece, h, other])
            each(C, wait)
        if piece_blocks:
            permute(piece)

    def g_step(n, carry):
        piece, h = nth(n, g_parts)
        arrived(g_buf.at[g_rows(piece, h, c)], gz_recv.at[piece, h])
        each(C, lambda m: g_pass(piece, h, m).start())
        issue(n + WINDOW)

        @pl.when(jnp.logical_and(h == 0, n > 0))
        def _():
            g_whole(jnp.right_shift(n, log2(g_parts)) - 1)
        return carry

    def r_arrived(m):
        q = wrap(me + m, Q)
        arrived(ring.at[q], r_recv.at[q])

    each(Q, r_arrived)
    lane = iota((1, kept), 1)
    begin = jnp.zeros((1, kept), I32)
    half = jnp.zeros((1, kept), I32)
    for q in range(Q):
        mine = jnp.right_shift(lane, log2(per_q)) == q
        begin = jnp.where(mine, ring[q, 0:1, :], begin)
        half = jnp.where(mine, ring[q, 1:2, :], half)
    fold = LANES // kr
    high_rows = kept // fold
    shape = (high_rows, LANES)
    wide_lane = iota(shape, 1)
    at_i = jnp.bitwise_and(wide_lane, kr - 1)
    group = jnp.right_shift(wide_lane, log2(kr))

    def down(vector):
        plain[...] = jnp.broadcast_to(vector, (kept, kept)).T
        got = plain[pl.ds(0, high_rows, stride=fold), :]
        for f in range(1, fold):
            got = jnp.where(group == f, plain[pl.ds(f, high_rows, stride=fold), :], got)
        return got

    row = jnp.bitwise_and(down(begin) + at_i * (2 * down(half) + 1), in_width - 1)
    piece_bits, context_bits = log2(rp), log2(C)
    sign = sign_of(jnp.bitwise_and(jnp.bitwise_and(jnp.right_shift(row, piece_bits), C - 1), c))
    held = (jnp.left_shift(jnp.right_shift(row, piece_bits + context_bits), piece_bits)
            + jnp.bitwise_and(row, rp - 1))
    local[5].wait()

    def expand(at, carry):
        here = pl.ds(pl.multiple_of(at * row_block, row_block), row_block)
        w = words[here, :]
        for b in range(BITS):
            signs[here, b * word_count:(b + 1) * word_count] = jnp.where(
                jnp.bitwise_and(w, 1 << b) != 0, -1.0, 1.0).astype(BF16)
        return carry

    lax.fori_loop(0, total_rows // row_block, expand, 0)
    local[3].wait()
    if piece_blocks:
        permute(s)
    lax.fori_loop(0, g_count, g_step, 0)
    g_whole(jnp.int32(S - 2))
    if not piece_blocks:
        lax.fori_loop(0, blocks, lambda at, _: (permute(at), 0)[1], 0)
    wide = min(WIDE, total_cols)

    def turn(at, carry):
        here = pl.ds(pl.multiple_of(at * wide, wide), wide)
        gt[:, here] = gp[here, :].T
        return carry

    lax.fori_loop(0, total_cols // wide, turn, 0)

    low_at = jnp.bitwise_and(held, row_block - 1)
    high_at = jnp.right_shift(held, log2(row_block))
    in_turn = jnp.bitwise_and(low_at, LANES - 1)
    which = jnp.right_shift(low_at, log2(LANES))
    sketch[...] = jnp.zeros(shape, F32)

    def add_block(at, values):
        if row_block < LANES:
            values = jnp.concatenate(
                [values, jnp.zeros((LANES - row_block, kept), F32)], axis=0)
        picked = jnp.zeros(shape, F32)
        for b in range(values.shape[0] // LANES):
            turned[b * LANES:(b + 1) * LANES, :] = values[b * LANES:(b + 1) * LANES, :].T
            found = None
            for f in range(fold):
                got = jnp.take_along_axis(
                    turned[pl.ds(b * LANES + f, high_rows, stride=fold), :], in_turn,
                    axis=1, mode="promise_in_bounds")
                found = got if found is None else jnp.where(group == f, got, found)
            picked = jnp.where(which == b, found, picked)
        sketch[...] += picked * sign_of(jnp.bitwise_and(high_at, at))

    def score_rows(row):
        here = pl.ds(pl.multiple_of(row, row_block), row_block)
        a = a_buf[here, :]
        total = jnp.zeros((row_block, kept), F32)
        for at in range(total_cols // wide):
            grad = jnp.dot(a, gt[:, at * wide:(at + 1) * wide], preferred_element_type=F32)
            high, low = split(grad)
            sign_here = signs[here, at * wide:(at + 1) * wide]
            high, low = high * sign_here, low * sign_here
            side = table[at * wide:(at + 1) * wide, :]
            total = total + jnp.dot(high, side, preferred_element_type=F32)
            total = total + jnp.dot(low, side, preferred_element_type=F32)
        got = jnp.dot(hada[...], jnp.concatenate(split(total), axis=1),
                      preferred_element_type=F32)
        add_block(jnp.right_shift(row, log2(row_block)), got[:, :kept] + got[:, kept:])

    local[4].wait()

    def a_step(n, carry):
        piece, h = nth(n - parts_of, parts_of)
        n_next = n - parts_of + 1
        next_piece, h_next = nth(n_next, parts_of)

        @pl.when(jnp.logical_and(n_next >= 0, n_next < a_count))
        def _():
            arrived(a_buf.at[a_rows(next_piece, h_next, k)], az_recv.at[next_piece, h_next])
            each(E, lambda m: a_pass(next_piece, h_next, m).start())
            issue(g_count + n_next + WINDOW)

        @pl.when(n >= parts_of)
        def _():
            def wait(m):
                other = wrap(k + m, E)
                arrived(a_buf.at[a_rows(piece, h, other)], ax_recv.at[piece, h, other])
            each(E, wait)

        score_rows(piece * rp + h * row_block)
        return carry

    lax.fori_loop(0, S * parts_of, a_step, 0)

    sketch[...] = sketch[...] * sign * scale

    per = high_rows // Q
    mine_at = s * Q + me

    def q_rows(q):
        return pl.ds(pl.multiple_of(q * per, per), per)

    def p_copy(m):
        t, q = member(m)
        return remote(sketch.at[q_rows(q)], parts.at[mine_at], p_send.at[0], p_recv.at[0],
                      spot(t, q))

    each(S * Q, lambda m: p_copy(m).start())
    parts[pl.ds(mine_at, 1)] = sketch[q_rows(me), :][None]
    local[6].wait()

    def sent(piece):
        for h in range(g_parts):
            each(C, lambda m: g_pass(piece, h, m).wait_send())
        for h in range(parts_of):
            each(E, lambda m: a_pass(piece, h, m).wait_send())

    pieces(sent)
    each(g_count + 1, lambda n: g_send(n - 1).wait_send())
    each(a_count + 1, lambda n: a_send(n - 1).wait_send())
    each(Q, lambda m: r_copy(m).wait_send())
    others = pl.ds(0, S * Q - 1)
    arrived(parts.at[others], p_recv.at[0])
    nvl = val.shape[0]
    nv = nvl * S
    totals, squares = [], []
    for e in range(S):
        own = parts[e * Q]
        for q in range(1, Q):
            own = own + parts[e * Q + q]
        total = jnp.zeros((nvl, LANES), F32)
        for r in range(per):
            total = total + val[:, r * LANES:(r + 1) * LANES] * own[r:r + 1, :]
        totals.append(total)
        squares.append(jnp.sum(own * own, axis=0, keepdims=True))
    tall = jnp.concatenate(
        totals + squares + [jnp.zeros((LANES - nv - S, LANES), F32)], axis=0)
    line = jnp.sum(tall.T, axis=0, keepdims=True)
    sums[pl.ds(mine_at, 1)] = jnp.broadcast_to(line, (8, LANES))[None]

    def s_copy(m):
        t, q = member(m)
        return remote(sums.at[mine_at], sums.at[mine_at], s_send.at[0], s_recv.at[0],
                      spot(t, q))

    each(S * Q, lambda m: s_copy(m).start())

    arrived(sums.at[others], s_recv.at[0])
    norm = None
    for t in range(S):
        line = sums[t * Q]
        for q in range(1, Q):
            line = line + sums[t * Q + q]
        if t == 0:
            at_norm = iota((1, LANES), 1) == nv + s
            norm = jnp.sum(jnp.where(at_norm, line[0:1, :], 0.0), axis=1, keepdims=True)
            norm = jnp.sqrt(norm + 1e-06)
        mine = pltpu.roll(line, wrap(LANES - s * nvl, LANES), axis=1)
        out[0:1, t * nvl:(t + 1) * nvl] = mine[0:1, :nvl] / norm
    arrived(parts.at[others], p_send.at[0])
    arrived(sums.at[others], s_send.at[0])


def body(activations, out_grads, sign_bits, keep_cols, row_start, row_step, val_sketch):
    S, C, E = lax.axis_size("sketch"), lax.axis_size("context"), lax.axis_size("example")
    Q = C * E
    rp, tokens = activations.shape[1:]
    gp_len = out_grads.shape[1]
    local_rows, local_cols = S * rp, S * gp_len
    in_width, out_width = local_rows * C, local_cols * E
    kept = keep_cols.shape[0]
    keep = val_sketch.shape[1] * Q
    kr = keep // kept
    nv = val_sketch.shape[0] * S
    words = sign_bits.reshape(local_rows, -1)
    row_block = min(ROWS, rp)
    parts_of = rp // row_block
    a_count = (S - 1) * parts_of
    g_parts = 2 if (gp_len // C) % 64 == 0 else 1
    g_count = (S - 1) * g_parts
    hbm = pl.BlockSpec(memory_space=pl.ANY)
    dma = pltpu.SemaphoreType.DMA
    block = min(WIDE, local_cols)
    return pl.pallas_call(
        functools.partial(
            kernel, (S, C, E), 1.0 / (math.sqrt(in_width) * math.sqrt(out_width)), kr),
        out_shape=jax.ShapeDtypeStruct((1, nv), F32),
        in_specs=[hbm] * 7,
        out_specs=pl.BlockSpec(memory_space=pltpu.VMEM),
        scratch_shapes=[
            pltpu.VMEM((local_rows, tokens), BF16),
            pltpu.VMEM((local_cols, tokens), BF16),
            pltpu.VMEM((local_cols, tokens), BF16),
            pltpu.VMEM((tokens, local_cols), BF16),
            pltpu.VMEM((local_cols, kept), BF16),
            pltpu.VMEM((block, block), BF16),
            pltpu.VMEM((row_block, row_block), BF16),
            pltpu.VMEM((local_rows, local_cols), BF16),
            pltpu.VMEM(words.shape, I32),
            pltpu.VMEM((1, kept), I32),
            pltpu.VMEM((1, kept // Q), I32),
            pltpu.VMEM((1, kept // Q), I32),
            pltpu.VMEM(val_sketch.shape, F32),
            pltpu.VMEM((max(row_block, LANES), LANES), F32),
            pltpu.VMEM((kept, kept), I32),
            pltpu.VMEM((Q, 8, kept), I32),
            pltpu.VMEM((keep // LANES, LANES), F32),
            pltpu.VMEM((S * Q, keep // LANES // Q, LANES), F32),
            pltpu.VMEM((S * Q, 8, LANES), F32),
            dma((7,)),
            dma((g_count,)), dma((S, g_parts)), dma((a_count,)), dma((S, parts_of)),
            dma((S, g_parts, C)), dma((S, g_parts, C)),
            dma((S, parts_of, E)), dma((S, parts_of, E)),
            dma((Q,)), dma((Q,)),
            dma((1,)), dma((1,)), dma((1,)), dma((1,)),
        ],
        compiler_params=pltpu.CompilerParams(
            collective_id=0, has_side_effects=True, vmem_limit_bytes=60 * 2**20),
        cost_estimate=pl.CostEstimate(
            flops=2 * local_rows * local_cols * (tokens + 2 * kept),
            bytes_accessed=2 * (local_rows + local_cols) * tokens, transcendentals=0),
        name="scores",
    )(activations, out_grads, words, keep_cols[None], row_start[None], row_step[None], val_sketch)


def solution(mesh):
    placed = (
        P("groups", ("sketch", "context"), None),
        P("groups", ("sketch", "example"), None),
        P(None, "context", None, "example", None),
        P(),
        P(("context", "example")),
        P(("context", "example")),
        P("sketch", ("context", "example")),
    )
    return jax.shard_map(
        body, mesh=mesh, in_specs=placed, out_specs=P(("groups", "sketch"), None), check_vma=False
    )
```

```python
import functools
import math

import jax
import jax.numpy as jnp
from jax import lax
from jax.experimental import pallas as pl
from jax.experimental.pallas import tpu as pltpu
from jax.sharding import PartitionSpec as P

MESH = pl.DeviceIdType.MESH
F32 = jnp.float32
BF16 = jnp.bfloat16
I32 = jnp.int32
LANES = 128
BITS = 16
ROWS = 256
WIDE = 512
WINDOW = 8


def log2(n):
    return n.bit_length() - 1


def sign_of(common):
    for shift in (16, 8, 4, 2, 1):
        common = jnp.bitwise_xor(common, jnp.right_shift(common, shift))
    return (1 - 2 * jnp.bitwise_and(common, 1)).astype(F32)


def iota(shape, axis):
    return lax.broadcasted_iota(I32, shape, axis)


def split(values):
    high = values.astype(BF16)
    return high, (values - high.astype(F32)).astype(BF16)


def place(s, c, k):
    return {"sketch": s, "context": c, "example": k}


def each(count, step):
    if count <= 16:
        for at in range(1, count):
            step(at)
    else:
        lax.fori_loop(1, count, lambda at, _: (step(at), 0)[1], 0)


def wrap(at, size):
    return jnp.bitwise_and(at, size - 1)


def kernel(sizes, scale, kr, act, grads, words_in, columns_in, begin_in, half_in, val_in, out,
           a_buf, g_buf, gp, gt, table, perm, hada, signs, words, columns, begins, halves, val,
           turned, plain, ring, sketch, parts, sums,
           own_sem, gz_send, gz_recv, az_send, az_recv, gx_send, gx_recv, ax_send, ax_recv,
           r_send, r_recv, p_send, p_recv, s_send, s_recv):
    S, C, E = sizes
    Q = C * E
    s, c, k = lax.axis_index("sketch"), lax.axis_index("context"), lax.axis_index("example")
    me = c * E + k
    rp, gp_len = act.shape[1], grads.shape[1]
    gh = gp_len // C
    g_parts = 2 if gh % 64 == 0 else 1
    gq = gh // g_parts
    row_block = min(ROWS, rp)
    parts_of = rp // row_block
    ah = row_block // E
    total_rows, total_cols = a_buf.shape[0], g_buf.shape[0]
    in_width, out_width = total_rows * C, total_cols * E
    word_count = words.shape[1]
    kept = columns.shape[1]

    def member(m):
        m = jnp.int32(m)
        return wrap(s + jnp.right_shift(m, log2(Q)), S), wrap(me + m, Q)

    def spot(t, q):
        return place(t, jnp.right_shift(q, log2(E)), wrap(q, E))

    barrier = pltpu.get_barrier_semaphore()

    def greet(m):
        pl.semaphore_signal(barrier, inc=1, device_id=spot(*member(m)),
                            device_id_type=MESH)

    local = [
        pltpu.make_async_copy(src, dst, own_sem.at[at]) for at, (src, dst) in enumerate((
            (begin_in, begins), (half_in, halves), (columns_in, columns),
            (grads.at[s], g_buf.at[pl.ds(pl.multiple_of(s * gp_len, gp_len), gp_len)]),
            (act.at[s], a_buf.at[pl.ds(pl.multiple_of(s * rp, rp), rp)]),
            (words_in, words), (val_in, val)))
    ]
    each(S * Q, greet)
    for copy in local:
        copy.start()
    pl.semaphore_wait(barrier, S * Q - 1)

    def remote(src, dst, send, recv, target):
        return pltpu.make_async_remote_copy(
            src_ref=src, dst_ref=dst, send_sem=send, recv_sem=recv,
            device_id=target, device_id_type=MESH)

    g_count, a_count = (S - 1) * g_parts, (S - 1) * parts_of

    def g_rows(piece, h, part_at):
        return pl.ds(pl.multiple_of(piece * gp_len + part_at * gh + h * gq, gq), gq)

    def a_rows(piece, h, part_at):
        return pl.ds(pl.multiple_of(piece * rp + h * row_block + part_at * ah, ah), ah)

    def mate(n):
        far = S // 2 + jnp.right_shift(n, 1)
        near = jnp.right_shift(n + 1, 1)
        return jnp.bitwise_xor(s, jnp.where(jnp.bitwise_and(n, 1) == 0, far, near))

    def nth(n, parts_in):
        n = jnp.int32(n)
        return mate(jnp.right_shift(n, log2(parts_in))), wrap(n, parts_in)

    def g_send(n):
        t, h = nth(n, g_parts)
        return remote(grads.at[t, pl.ds(pl.multiple_of(c * gh + h * gq, gq), gq)],
                      g_buf.at[g_rows(s, h, c)], gz_send.at[n], gz_recv.at[s, h],
                      place(t, c, k))

    def a_send(n):
        t, h = nth(n, parts_of)
        return remote(act.at[t, pl.ds(pl.multiple_of(h * row_block + k * ah, ah), ah)],
                      a_buf.at[a_rows(s, h, k)], az_send.at[n], az_recv.at[s, h],
                      place(t, c, k))

    def g_pass(piece, h, m):
        rows = g_rows(piece, h, c)
        return remote(g_buf.at[rows], g_buf.at[rows], gx_send.at[piece, h, m],
                      gx_recv.at[piece, h, c], place(s, wrap(c + m, C), k))

    def a_pass(piece, h, m):
        rows = a_rows(piece, h, k)
        return remote(a_buf.at[rows], a_buf.at[rows], ax_send.at[piece, h, m],
                      ax_recv.at[piece, h, k], place(s, c, wrap(k + m, E)))

    def arrived(ref, sem):
        pltpu.make_async_copy(ref, ref, sem).wait()

    def pieces(step):
        each(S, lambda o: step(mate(jnp.int32(o - 1))))

    def issue(n):
        n = jnp.int32(n)

        @pl.when(n < g_count)
        def _():
            g_send(n).start()

        @pl.when(jnp.logical_and(n >= g_count, n < g_count + a_count))
        def _():
            a_send(n - g_count).start()

    lax.fori_loop(0, WINDOW, lambda n, _: (issue(n), 0)[1], 0)

    for copy in local[:2]:
        copy.wait()
    per_q = kept // Q
    ring[pl.ds(me, 1)] = jnp.zeros((1, 8, kept), I32)
    for q in range(Q):
        ring[me, 0:1, q * per_q:(q + 1) * per_q] = begins[...]
        ring[me, 1:2, q * per_q:(q + 1) * per_q] = halves[...]

    def r_copy(m):
        return remote(ring.at[me], ring.at[me], r_send.at[m], r_recv.at[me],
                      spot(s, wrap(me + m, Q)))

    each(Q, lambda m: r_copy(m).start())

    local[2].wait()
    width = out_width // kept
    kept_cols = columns[...] + iota((1, kept), 1) * width

    def tabulate(b, carry):
        at = iota((word_count, kept), 0) * BITS + b
        full = ((jnp.right_shift(at, log2(gp_len)) * E + k) * gp_len
                + jnp.bitwise_and(at, gp_len - 1))
        table[pl.ds(pl.multiple_of(b * word_count, word_count), word_count), :] = sign_of(
            jnp.bitwise_and(full, kept_cols)).astype(BF16)
        return carry

    lax.fori_loop(0, BITS, tabulate, 0)
    hada[...] = sign_of(jnp.bitwise_and(
        iota((row_block, row_block), 0), iota((row_block, row_block), 1))).astype(BF16)

    block = perm.shape[0]
    block_words = block // BITS
    blocks = total_cols // block
    row_at, col_at = iota((block, block), 0), iota((block, block), 1)
    source = (jnp.bitwise_and(row_at, block_words - 1) * BITS
              + jnp.right_shift(row_at, log2(block_words)))
    perm[...] = jnp.where(col_at == source, 1.0, 0.0).astype(BF16)

    def permute(at):
        rows = g_buf[pl.ds(pl.multiple_of(at * block, block), block), :]
        moved = jnp.dot(perm[...], rows, preferred_element_type=F32).astype(BF16)
        for b in range(BITS):
            gp[pl.ds(pl.multiple_of(b * word_count + at * block_words, block_words),
                     block_words), :] = moved[b * block_words:(b + 1) * block_words]

    piece_blocks = block == gp_len

    def g_whole(n):
        piece = mate(n)
        for h in range(g_parts):
            def wait(m):
                other = wrap(c + m, C)
                arrived(g_buf.at[g_rows(piece, h, other)], gx_recv.at[piece, h, other])
            each(C, wait)
        if piece_blocks:
            permute(piece)

    def g_step(n, carry):
        piece, h = nth(n, g_parts)
        arrived(g_buf.at[g_rows(piece, h, c)], gz_recv.at[piece, h])
        each(C, lambda m: g_pass(piece, h, m).start())
        issue(n + WINDOW)

        @pl.when(jnp.logical_and(h == 0, n > 0))
        def _():
            g_whole(jnp.right_shift(n, log2(g_parts)) - 1)
        return carry

    def r_arrived(m):
        q = wrap(me + m, Q)
        arrived(ring.at[q], r_recv.at[q])

    each(Q, r_arrived)
    lane = iota((1, kept), 1)
    begin = jnp.zeros((1, kept), I32)
    half = jnp.zeros((1, kept), I32)
    for q in range(Q):
        mine = jnp.right_shift(lane, log2(per_q)) == q
        begin = jnp.where(mine, ring[q, 0:1, :], begin)
        half = jnp.where(mine, ring[q, 1:2, :], half)
    fold = LANES // kr
    high_rows = kept // fold
    shape = (high_rows, LANES)
    wide_lane = iota(shape, 1)
    at_i = jnp.bitwise_and(wide_lane, kr - 1)
    group = jnp.right_shift(wide_lane, log2(kr))

    def down(vector):
        plain[...] = jnp.broadcast_to(vector, (kept, kept)).T
        got = plain[pl.ds(0, high_rows, stride=fold), :]
        for f in range(1, fold):
            got = jnp.where(group == f, plain[pl.ds(f, high_rows, stride=fold), :], got)
        return got

    row = jnp.bitwise_and(down(begin) + at_i * (2 * down(half) + 1), in_width - 1)
    piece_bits, context_bits = log2(rp), log2(C)
    sign = sign_of(jnp.bitwise_and(jnp.bitwise_and(jnp.right_shift(row, piece_bits), C - 1), c))
    held = (jnp.left_shift(jnp.right_shift(row, piece_bits + context_bits), piece_bits)
            + jnp.bitwise_and(row, rp - 1))
    local[5].wait()

    def expand(at, carry):
        here = pl.ds(pl.multiple_of(at * row_block, row_block), row_block)
        w = words[here, :]
        for b in range(BITS):
            signs[here, b * word_count:(b + 1) * word_count] = jnp.where(
                jnp.bitwise_and(w, 1 << b) != 0, -1.0, 1.0).astype(BF16)
        return carry

    lax.fori_loop(0, total_rows // row_block, expand, 0)
    local[3].wait()
    if piece_blocks:
        permute(s)
    lax.fori_loop(0, g_count, g_step, 0)
    g_whole(jnp.int32(S - 2))
    if not piece_blocks:
        lax.fori_loop(0, blocks, lambda at, _: (permute(at), 0)[1], 0)
    wide = min(WIDE, total_cols)

    def turn(at, carry):
        here = pl.ds(pl.multiple_of(at * wide, wide), wide)
        gt[:, here] = gp[here, :].T
        return carry

    lax.fori_loop(0, total_cols // wide, turn, 0)

    low_at = jnp.bitwise_and(held, row_block - 1)
    high_at = jnp.right_shift(held, log2(row_block))
    in_turn = jnp.bitwise_and(low_at, LANES - 1)
    which = jnp.right_shift(low_at, log2(LANES))
    sketch[...] = jnp.zeros(shape, F32)

    def add_block(at, values):
        if row_block < LANES:
            values = jnp.concatenate(
                [values, jnp.zeros((LANES - row_block, kept), F32)], axis=0)
        picked = jnp.zeros(shape, F32)
        for b in range(values.shape[0] // LANES):
            turned[b * LANES:(b + 1) * LANES, :] = values[b * LANES:(b + 1) * LANES, :].T
            found = None
            for f in range(fold):
                got = jnp.take_along_axis(
                    turned[pl.ds(b * LANES + f, high_rows, stride=fold), :], in_turn,
                    axis=1, mode="promise_in_bounds")
                found = got if found is None else jnp.where(group == f, got, found)
            picked = jnp.where(which == b, found, picked)
        sketch[...] += picked * sign_of(jnp.bitwise_and(high_at, at))

    def score_rows(row):
        here = pl.ds(pl.multiple_of(row, row_block), row_block)
        a = a_buf[here, :]
        total = jnp.zeros((row_block, kept), F32)
        for at in range(total_cols // wide):
            grad = jnp.dot(a, gt[:, at * wide:(at + 1) * wide], preferred_element_type=F32)
            high, low = split(grad)
            sign_here = signs[here, at * wide:(at + 1) * wide]
            high, low = high * sign_here, low * sign_here
            side = table[at * wide:(at + 1) * wide, :]
            total = total + jnp.dot(high, side, preferred_element_type=F32)
            total = total + jnp.dot(low, side, preferred_element_type=F32)
        got = jnp.dot(hada[...], jnp.concatenate(split(total), axis=1),
                      preferred_element_type=F32)
        add_block(jnp.right_shift(row, log2(row_block)), got[:, :kept] + got[:, kept:])

    local[4].wait()

    def a_step(n, carry):
        piece, h = nth(n - parts_of, parts_of)
        n_next = n - parts_of + 1
        next_piece, h_next = nth(n_next, parts_of)

        @pl.when(jnp.logical_and(n_next >= 0, n_next < a_count))
        def _():
            arrived(a_buf.at[a_rows(next_piece, h_next, k)], az_recv.at[next_piece, h_next])
            each(E, lambda m: a_pass(next_piece, h_next, m).start())
            issue(g_count + n_next + WINDOW)

        @pl.when(n >= parts_of)
        def _():
            def wait(m):
                other = wrap(k + m, E)
                arrived(a_buf.at[a_rows(piece, h, other)], ax_recv.at[piece, h, other])
            each(E, wait)

        score_rows(piece * rp + h * row_block)
        return carry

    lax.fori_loop(0, S * parts_of, a_step, 0)

    sketch[...] = sketch[...] * sign * scale

    per = high_rows // Q
    mine_at = s * Q + me

    def q_rows(q):
        return pl.ds(pl.multiple_of(q * per, per), per)

    def p_copy(m):
        t, q = member(m)
        return remote(sketch.at[q_rows(q)], parts.at[mine_at], p_send.at[0], p_recv.at[0],
                      spot(t, q))

    each(S * Q, lambda m: p_copy(m).start())
    parts[pl.ds(mine_at, 1)] = sketch[q_rows(me), :][None]
    local[6].wait()

    def sent(piece):
        for h in range(g_parts):
            each(C, lambda m: g_pass(piece, h, m).wait_send())
        for h in range(parts_of):
            each(E, lambda m: a_pass(piece, h, m).wait_send())

    pieces(sent)
    each(g_count + 1, lambda n: g_send(n - 1).wait_send())
    each(a_count + 1, lambda n: a_send(n - 1).wait_send())
    each(Q, lambda m: r_copy(m).wait_send())
    others = pl.ds(0, S * Q - 1)
    arrived(parts.at[others], p_recv.at[0])
    nvl = val.shape[0]
    nv = nvl * S
    totals, squares = [], []
    for e in range(S):
        own = parts[e * Q]
        for q in range(1, Q):
            own = own + parts[e * Q + q]
        total = jnp.zeros((nvl, LANES), F32)
        for r in range(per):
            total = total + val[:, r * LANES:(r + 1) * LANES] * own[r:r + 1, :]
        totals.append(total)
        squares.append(jnp.sum(own * own, axis=0, keepdims=True))
    tall = jnp.concatenate(
        totals + squares + [jnp.zeros((LANES - nv - S, LANES), F32)], axis=0)
    line = jnp.sum(tall.T, axis=0, keepdims=True)
    sums[pl.ds(mine_at, 1)] = jnp.broadcast_to(line, (8, LANES))[None]

    def s_copy(m):
        t, q = member(m)
        return remote(sums.at[mine_at], sums.at[mine_at], s_send.at[0], s_recv.at[0],
                      spot(t, q))

    each(S * Q, lambda m: s_copy(m).start())

    arrived(sums.at[others], s_recv.at[0])
    norm = None
    for t in range(S):
        line = sums[t * Q]
        for q in range(1, Q):
            line = line + sums[t * Q + q]
        if t == 0:
            at_norm = iota((1, LANES), 1) == nv + s
            norm = jnp.sum(jnp.where(at_norm, line[0:1, :], 0.0), axis=1, keepdims=True)
            norm = jnp.sqrt(norm + 1e-06)
        mine = pltpu.roll(line, wrap(LANES - s * nvl, LANES), axis=1)
        out[0:1, t * nvl:(t + 1) * nvl] = mine[0:1, :nvl] / norm
    arrived(parts.at[others], p_send.at[0])
    arrived(sums.at[others], s_send.at[0])


def body(activations, out_grads, sign_bits, keep_cols, row_start, row_step, val_sketch):
    S, C, E = lax.axis_size("sketch"), lax.axis_size("context"), lax.axis_size("example")
    Q = C * E
    rp, tokens = activations.shape[1:]
    gp_len = out_grads.shape[1]
    local_rows, local_cols = S * rp, S * gp_len
    in_width, out_width = local_rows * C, local_cols * E
    kept = keep_cols.shape[0]
    keep = val_sketch.shape[1] * Q
    kr = keep // kept
    nv = val_sketch.shape[0] * S
    words = sign_bits.reshape(local_rows, -1)
    row_block = min(ROWS, rp)
    parts_of = rp // row_block
    a_count = (S - 1) * parts_of
    g_parts = 2 if (gp_len // C) % 64 == 0 else 1
    g_count = (S - 1) * g_parts
    hbm = pl.BlockSpec(memory_space=pl.ANY)
    dma = pltpu.SemaphoreType.DMA
    block = min(WIDE, local_cols)
    return pl.pallas_call(
        functools.partial(
            kernel, (S, C, E), 1.0 / (math.sqrt(in_width) * math.sqrt(out_width)), kr),
        out_shape=jax.ShapeDtypeStruct((1, nv), F32),
        in_specs=[hbm] * 7,
        out_specs=pl.BlockSpec(memory_space=pltpu.VMEM),
        scratch_shapes=[
            pltpu.VMEM((local_rows, tokens), BF16),
            pltpu.VMEM((local_cols, tokens), BF16),
            pltpu.VMEM((local_cols, tokens), BF16),
            pltpu.VMEM((tokens, local_cols), BF16),
            pltpu.VMEM((local_cols, kept), BF16),
            pltpu.VMEM((block, block), BF16),
            pltpu.VMEM((row_block, row_block), BF16),
            pltpu.VMEM((local_rows, local_cols), BF16),
            pltpu.VMEM(words.shape, I32),
            pltpu.VMEM((1, kept), I32),
            pltpu.VMEM((1, kept // Q), I32),
            pltpu.VMEM((1, kept // Q), I32),
            pltpu.VMEM(val_sketch.shape, F32),
            pltpu.VMEM((max(row_block, LANES), LANES), F32),
            pltpu.VMEM((kept, kept), I32),
            pltpu.VMEM((Q, 8, kept), I32),
            pltpu.VMEM((keep // LANES, LANES), F32),
            pltpu.VMEM((S * Q, keep // LANES // Q, LANES), F32),
            pltpu.VMEM((S * Q, 8, LANES), F32),
            dma((7,)),
            dma((g_count,)), dma((S, g_parts)), dma((a_count,)), dma((S, parts_of)),
            dma((S, g_parts, C)), dma((S, g_parts, C)),
            dma((S, parts_of, E)), dma((S, parts_of, E)),
            dma((Q,)), dma((Q,)),
            dma((1,)), dma((1,)), dma((1,)), dma((1,)),
        ],
        compiler_params=pltpu.CompilerParams(
            collective_id=0, has_side_effects=True, vmem_limit_bytes=60 * 2**20),
        cost_estimate=pl.CostEstimate(
            flops=2 * local_rows * local_cols * (tokens + 2 * kept),
            bytes_accessed=2 * (local_rows + local_cols) * tokens, transcendentals=0),
        name="scores",
    )(activations, out_grads, words, keep_cols[None], row_start[None], row_step[None], val_sketch)


def solution(mesh):
    placed = (
        P("groups", ("sketch", "context"), None),
        P("groups", ("sketch", "example"), None),
        P(None, "context", None, "example", None),
        P(),
        P(("context", "example")),
        P(("context", "example")),
        P("sketch", ("context", "example")),
    )
    return jax.shard_map(
        body, mesh=mesh, in_specs=placed, out_specs=P(("groups", "sketch"), None), check_vma=False
    )
```
